32 devices in a mesh: tgt: 8 (over z, x), sec: 4 (over y, core).
Axes of the slice: x: 2, y: 2, z: 4, core: 2. Of those that a mesh axis runs over, the one named last changes fastest.
Arguments:
- queries: bfloat16 [2048, 4096], P('tgt', 'sec'), may hold values from -210 to 210
- key_values: bfloat16 [2, 2048, 4096], P(None, 'tgt', 'sec'), may hold values from -6.06 to 6.06
- grad_out: bfloat16 [2048, 4096], P('tgt', 'sec'), may hold values from -192 to 192
- block_ids: int32 [16, 4], P('tgt'), may hold values from 0 to 15, as said below
- block_count: int32 [16], P('tgt'), may hold values from 1 to 4, as said below
- kv_weight: bfloat16 [2, 4096, 4096], P(None, 'tgt', 'sec'), may hold values from -0.0625 to 0.0625
Outputs:
- grad_queries: bfloat16 [2048, 4096], P('tgt', 'sec')
- grad_memory: bfloat16 [2048, 4096], P('tgt', 'sec')
The draws below stay inside these ranges and needn't reach their ends.
Inputs may be any that keep to these rules, and one draw needn't show every extreme that they name: `block_ids`: target block i, which lies in the rows of index t = i // 2 of tgt, lists only source blocks in the rows of indices t - 1, t and t + 1; its first entry is block i itself; its live entries are distinct; entries past its count repeat block i. `block_count`: every eighth block, starting at block 3, has all slots live.
All inputs are finite; a program needn't handle non-finite values.
Results may differ from the reference program's by a relative error of at most 0.013.
Values may be sent and summed in bfloat16 or wider, within the bound.
No kernel may reach another device: no remote copies, remote signals or barrier semaphores. Data moves between devices by JAX's collectives and lax.ppermute only.
A program may use at most 128 MiB of HBM per device.

```python
import jax
import jax.numpy as jnp
from jax import lax

D = 4096
HEADS = 64
HEAD_DIM = 64
BLOCK = 128
SLOTS = 4
ROWS_DEV = 256
ROWS = 2048
N_SEC = 4


def base_pairs(key):
    width = HEADS * HEAD_DIM
    values = jnp.clip(jax.random.normal(jax.random.fold_in(key, 31), (2, ROWS, width), jnp.float32), -6.0, 6.0)
    return values


def draw_key_values(key, part):
    return base_pairs(key).astype(jnp.bfloat16)


def draw_queries(key, part):
    width = HEADS * HEAD_DIM
    drawn = jnp.clip(jax.random.normal(jax.random.fold_in(key, 32), (ROWS, width), jnp.float32), -6.0, 6.0)
    return drawn.astype(jnp.bfloat16)


def align_lists(key):
    nblocks = ROWS // BLOCK
    per_device = ROWS_DEV // BLOCK
    counts = jax.random.randint(jax.random.fold_in(key, 21), (nblocks,), 1, SLOTS + 1)
    block_pos = jnp.arange(nblocks)
    counts = jnp.where(block_pos % 8 == 3, SLOTS, counts).astype(jnp.int32)
    device_of = block_pos // per_device
    first = (device_of - 1) * per_device
    candidate = first[:, None] + jnp.arange(3 * per_device)[None, :]
    usable = (candidate >= 0) & (candidate < nblocks) & (candidate != block_pos[:, None])
    rank_keys = jax.random.randint(jax.random.fold_in(key, 22), (nblocks, 3 * per_device), 0, 1000)
    rank_keys = rank_keys * (4 * per_device) + jnp.arange(3 * per_device)[None, :]
    rank_keys = jnp.where(usable, rank_keys, 100000000)
    order = jnp.argsort(rank_keys, axis=1, stable=True)
    others = jnp.take_along_axis(candidate, order[:, :SLOTS - 1], axis=1)
    listed = jnp.concatenate([block_pos[:, None], others], axis=1)
    slot_pos = jnp.arange(SLOTS)[None, :]
    listed = jnp.where(slot_pos < counts[:, None], listed, block_pos[:, None])
    return (listed.astype(jnp.int32), counts)


def draw_block_ids(key, part):
    return align_lists(key)[0]


def draw_block_count(key, part):
    return align_lists(key)[1]


def block_scale(key, dims, shards, least, largest):
    level = 1.0
    for position, parts in shards:
        draws = jax.random.uniform(jax.random.fold_in(jax.random.fold_in(key, 6), position), (parts,), jnp.float32, least / len(shards), largest / len(shards))
        level = level * jnp.repeat(jnp.exp(draws), dims[position] // parts).reshape((-1,) + (1,) * (len(dims) - 1 - position))
    return level


def noise(key, dims, spread, limit, pieces=(), dtype=jnp.bfloat16):
    result = jax.random.normal(key, dims, jnp.float32) * spread
    if len(pieces) > 0:
        result = block_scale(key, dims, pieces, -0.22, 0.18) * result
    return jnp.clip(result, min=-limit, max=limit).astype(dtype)


def setup_inputs(seed: int = 0) -> dict:
    key_list = jax.random.split(jax.random.key(seed), 7)
    queries = draw_queries(jax.random.fold_in(key_list[6], 71), 0)
    key_values = draw_key_values(jax.random.fold_in(key_list[6], 71), 0)
    grad_out = noise(key_list[2], (ROWS, HEADS * HEAD_DIM), 32.0, 192.0, ((0, 8), (1, 4)))
    block_ids = draw_block_ids(jax.random.fold_in(key_list[6], 71), 0)
    block_count = draw_block_count(jax.random.fold_in(key_list[6], 71), 0)
    kv_weight = noise(key_list[5], (2, D, HEADS * HEAD_DIM), (2 * HEADS * HEAD_DIM) ** -0.5, 0.0625, ((1, 8), (2, 4)))
    return dict(queries=queries, key_values=key_values, grad_out=grad_out, block_ids=block_ids, block_count=block_count, kv_weight=kv_weight)


def reference(queries, key_values, grad_out, block_ids, block_count, kv_weight):
    total_rows = queries.shape[0]
    width = queries.shape[1]
    heads = width // HEAD_DIM
    nblocks = total_rows // BLOCK
    kv_blocks = key_values.reshape(2, nblocks, BLOCK, width)

    def block_step(carry, inputs):
        query_block, upstream_block, listed, count = inputs
        picked = kv_blocks[:, listed]
        key_rows = picked[0].reshape(SLOTS * BLOCK, heads, HEAD_DIM).astype(jnp.float32)
        value_rows = picked[1].reshape(SLOTS * BLOCK, heads, HEAD_DIM).astype(jnp.float32)
        query_rows = query_block.reshape(BLOCK, heads, HEAD_DIM).astype(jnp.float32)
        upstream = upstream_block.reshape(BLOCK, heads, HEAD_DIM).astype(jnp.float32)
        key_live = jnp.repeat(jnp.arange(SLOTS) < count, BLOCK)
        scores = 0.125 * jnp.einsum("qhd,khd->hqk", query_rows, key_rows)
        scores = jnp.where(key_live[None, None, :], scores, -jnp.inf)
        row_max = jnp.max(scores, axis=-1, keepdims=True)
        expo = jnp.exp(scores - row_max)
        probs = expo / jnp.sum(expo, axis=-1, keepdims=True)
        probs_half = probs.astype(jnp.bfloat16).astype(jnp.float32)
        attended = jnp.einsum("hqk,khd->qhd", probs_half, value_rows)
        delta = jnp.sum(upstream * attended, axis=-1)
        grad_probs = jnp.einsum("qhd,khd->hqk", upstream, value_rows)
        grad_scores = probs * (grad_probs - jnp.transpose(delta)[:, :, None])
        grad_half = grad_scores.astype(jnp.bfloat16).astype(jnp.float32)
        grad_query = 0.125 * jnp.einsum("hqk,khd->qhd", grad_half, key_rows)
        grad_key = 0.125 * jnp.einsum("hqk,qhd->khd", grad_half, query_rows)
        grad_value = jnp.einsum("hqk,qhd->khd", probs_half, upstream)
        pair = jnp.stack([grad_key, grad_value]).reshape(2, SLOTS, BLOCK, width)
        carry = carry.at[:, listed].add(pair)
        return carry, grad_query.reshape(BLOCK, width).astype(jnp.bfloat16)

    start = jnp.zeros((2, nblocks, BLOCK, width), jnp.float32)
    inputs = (queries.reshape(nblocks, BLOCK, width), grad_out.reshape(nblocks, BLOCK, width),
              block_ids.astype(jnp.int32), block_count.astype(jnp.int32))
    summed, grad_blocks = lax.scan(block_step, start, inputs)
    grads_half = summed.reshape(2, total_rows, width).astype(jnp.bfloat16)
    group_width = width // N_SEC
    memory = jnp.zeros((total_rows, kv_weight.shape[1]), jnp.float32)
    for group in range(N_SEC):
        left_part = grads_half[:, :, group * group_width:(group + 1) * group_width]
        right_part = kv_weight[:, :, group * group_width:(group + 1) * group_width]
        head_part = jnp.dot(left_part[0], right_part[0].T, preferred_element_type=jnp.float32)
        head_part = head_part + jnp.dot(left_part[1], right_part[1].T, preferred_element_type=jnp.float32)
        head_half = lax.optimization_barrier(head_part.astype(jnp.bfloat16))
        memory = memory + head_half.astype(jnp.float32)
    return grad_blocks.reshape(total_rows, width), memory.astype(jnp.bfloat16)
```

```python
import functools
import math

import jax
import jax.numpy as jnp
from jax import lax
from jax.experimental import pallas as pl
from jax.experimental.pallas import tpu as pltpu
from jax.sharding import PartitionSpec as P

HEAD_DIM = 64
BLOCK = 128
SLOTS = 4
GROUP = 4
AXES = ("tgt", "sec")
SCALE = 0.125
NT = (((1,), (1,)), ((), ()))
TN = (((0,), (0,)), ((), ()))


def send(block, route):
    rows, secs = lax.axis_size("tgt"), lax.axis_size("sec")
    pairs = []
    for t in range(rows):
        for s in range(secs):
            target = route(t, s)
            if target is not None and 0 <= target[0] < rows:
                pairs.append((t * secs + s, target[0] * secs + target[1]))
    return lax.ppermute(block, AXES, pairs)


def swap(block, a):
    return send(block, lambda t, s: (t ^ a, s))


def attend_kernel(meta, pos, *refs):
    pairs, targets = refs[:GROUP], refs[GROUP : 2 * GROUP]
    refs = refs[2 * GROUP :]
    n_halo = (len(refs) - GROUP - 2 - 10) // 2
    halos, refs = refs[:n_halo], refs[n_halo:]
    dq_outs, refs = refs[:GROUP], refs[GROUP:]
    inner, edge, refs = refs[0], refs[1], refs[2:]
    backs, refs = refs[:n_halo], refs[n_halo:]
    keys, values, rows, ups, acc, dq_all, kg, vg, qm, om = refs
    per_dev, width = pairs[0].shape[1], pairs[0].shape[3]
    heads = width // HEAD_DIM
    own = GROUP * per_dev
    here, start = pos[0], pos[1]
    for a in range(GROUP):
        place = pl.ds((here ^ a) * per_dev, per_dev)
        block = (per_dev, BLOCK, width)
        rows[place] = targets[a][: per_dev * BLOCK].reshape(block)
        ups[place] = targets[a][per_dev * BLOCK : 2 * per_dev * BLOCK].reshape(block)
        keys[place] = pairs[a][0]
        values[place] = pairs[a][1]
    for n in range(n_halo):
        part = slice(own + n * per_dev, own + (n + 1) * per_dev)
        keys[part] = halos[n][0]
        values[part] = halos[n][1]
    acc[...] = jnp.zeros_like(acc)
    lane_head = lax.broadcasted_iota(jnp.int32, (BLOCK, width), 1) // HEAD_DIM
    key_row = lax.broadcasted_iota(jnp.int32, (SLOTS * BLOCK, heads * BLOCK), 0)

    def step(i, carry):
        a = here ^ (i // per_dev)
        r = i % per_dev
        count = meta[a, r, SLOTS]
        ids = [meta[a, r, s] for s in range(SLOTS)]
        for s in range(SLOTS):
            kg[s * BLOCK : (s + 1) * BLOCK] = keys[ids[s]]
            vg[s * BLOCK : (s + 1) * BLOCK] = values[ids[s]]
        q, o = rows[i], ups[i]
        for h in range(heads):
            qm[h * BLOCK : (h + 1) * BLOCK] = jnp.where(lane_head == h, q, 0)
            om[h * BLOCK : (h + 1) * BLOCK] = jnp.where(lane_head == h, o, 0)
        scores = lax.dot_general(kg[...], qm[...], NT, preferred_element_type=jnp.float32)
        scores = jnp.where(key_row < count * BLOCK, scores, -jnp.inf)
        top = jnp.max(scores, axis=0, keepdims=True)
        expo = jnp.exp2((scores - top) * (SCALE * math.log2(math.e)))
        probs = expo * (1.0 / jnp.sum(expo, axis=0, keepdims=True))
        probs_half = probs.astype(jnp.bfloat16)
        grad_probs = lax.dot_general(vg[...], om[...], NT, preferred_element_type=jnp.float32)
        delta = jnp.sum(probs_half.astype(jnp.float32) * grad_probs, axis=0, keepdims=True)
        grad_half = (probs * (grad_probs - delta)).astype(jnp.bfloat16)
        grad_value = jnp.dot(probs_half, om[...], preferred_element_type=jnp.float32)
        grad_key = SCALE * jnp.dot(grad_half, qm[...], preferred_element_type=jnp.float32)
        for s in range(SLOTS):
            part = slice(s * BLOCK, (s + 1) * BLOCK)
            acc[0, ids[s]] += grad_key[part]
            acc[1, ids[s]] += grad_value[part]
        flipped = lax.dot_general(kg[...], grad_half, TN, preferred_element_type=jnp.float32)
        flipped = jnp.concatenate(
            [
                flipped[h * HEAD_DIM : (h + 1) * HEAD_DIM, h * BLOCK : (h + 1) * BLOCK]
                for h in range(heads)
            ],
            axis=0,
        )
        dq_all[i] = (SCALE * flipped.T).astype(jnp.bfloat16)
        return carry

    lax.fori_loop(0, own, step, 0)
    for a in range(GROUP):
        dq_outs[a][...] = dq_all[pl.ds((here ^ a) * per_dev, per_dev)]
    half = jnp.bfloat16
    for p in range(GROUP):
        m = lax.rem(start + 1 + p, GROUP)
        taken = acc[:, pl.ds(m * per_dev, per_dev)]
        if p < GROUP - n_halo:
            inner[:, p * per_dev : (p + 1) * per_dev] = taken.astype(half)
        else:
            p -= GROUP - n_halo
            edge[:, p * per_dev : (p + 1) * per_dev] = taken
    for n in range(n_halo):
        part = slice(own + n * per_dev, own + (n + 1) * per_dev)
        backs[n][...] = acc[:, part].astype(half)


def attend(meta, pos, pairs, targets, halos):
    _, per_dev, _, width = pairs[0].shape
    n_halo = len(halos)
    own = GROUP * per_dev
    total = own + n_halo * per_dev
    heads = width // HEAD_DIM
    half = jnp.bfloat16
    block = (BLOCK, width)
    shapes = (
        [jax.ShapeDtypeStruct((per_dev,) + block, half)] * GROUP
        + [
            jax.ShapeDtypeStruct((2, own - n_halo * per_dev) + block, half),
            jax.ShapeDtypeStruct((2, n_halo * per_dev) + block, jnp.float32),
        ]
        + [jax.ShapeDtypeStruct((2, per_dev) + block, half)] * n_halo
    )
    scratch = [
        pltpu.VMEM((total,) + block, half),
        pltpu.VMEM((total,) + block, half),
        pltpu.VMEM((own,) + block, half),
        pltpu.VMEM((own,) + block, half),
        pltpu.VMEM((2, total) + block, jnp.float32),
        pltpu.VMEM((own,) + block, half),
        pltpu.VMEM((SLOTS * BLOCK, width), half),
        pltpu.VMEM((SLOTS * BLOCK, width), half),
        pltpu.VMEM((heads * BLOCK, width), half),
        pltpu.VMEM((heads * BLOCK, width), half),
    ]
    whole = pl.BlockSpec(memory_space=pltpu.VMEM)
    scalars = pl.BlockSpec(memory_space=pltpu.SMEM)
    results = pl.pallas_call(
        attend_kernel,
        out_shape=shapes,
        in_specs=[scalars] * 2 + [whole] * (2 * GROUP + n_halo),
        out_specs=[whole] * len(shapes),
        scratch_shapes=scratch,
        compiler_params=pltpu.CompilerParams(vmem_limit_bytes=40 * 2**20),
        cost_estimate=pl.CostEstimate(
            flops=own * 10 * SLOTS * BLOCK * heads * BLOCK * width,
            bytes_accessed=8 * 2**20,
            transcendentals=own * SLOTS * heads * BLOCK * BLOCK,
        ),
        name="attend",
    )(meta, pos, *pairs, *targets, *halos)
    return results[:GROUP], results[GROUP], results[GROUP + 1], results[GROUP + 2 :]


def project_kernel(ranges, n_out, pos, *refs):
    inner, edge, refs = refs[:GROUP], refs[GROUP : 2 * GROUP], refs[2 * GROUP :]
    weights, refs = refs[: len(ranges)], refs[len(ranges) :]
    outs, (left, result) = refs[:n_out], refs[n_out:]
    width = inner[0].shape[3]
    n_inner, n_edge = inner[0].shape[1], edge[0].shape[1]
    per_dev = (n_inner + n_edge) // GROUP
    rows = per_dev * BLOCK
    depth = GROUP * width
    here, start, flip = pos[0], pos[1], pos[2]

    def step(j, carry):
        p = lax.rem(pos[3 + j] + (GROUP - 1) - start, GROUP) * per_dev

        def fill(sources, first):
            for a in range(GROUP):
                column = (here ^ a) * width
                for c in range(2):
                    piece = sources[a][c, pl.ds(p - first, per_dev)].reshape(rows, width)
                    left[:, pl.ds(pl.multiple_of(c * depth + column, width), width)] = piece

        @pl.when(p < n_inner)
        def _():
            fill(inner, 0)

        @pl.when(p >= n_inner)
        def _():
            fill(edge, n_inner)

        for weight, (k, first, size, column) in zip(weights, ranges):
            total = None
            for c in range(2):
                term = lax.dot_general(
                    left[:, c * depth : (c + 1) * depth],
                    weight[c, first : first + size],
                    NT,
                    preferred_element_type=jnp.float32,
                )
                total = term if total is None else total + term
            result[j, k, :, column : column + size] = total.astype(result.dtype)
        return carry

    lax.fori_loop(0, GROUP, step, 0)
    n_k = n_out // GROUP
    for j in range(GROUP):
        for k in range(n_k):
            outs[j * n_k + k][...] = result[j, (k ^ flip) if n_k == 2 else k]


def project(pos, inner, edge, weights, ranges):
    per_dev = (inner[0].shape[1] + edge[0].shape[1]) // GROUP
    rows = per_dev * BLOCK
    width = inner[0].shape[3]
    whole = pl.BlockSpec(memory_space=pltpu.VMEM)
    columns = max(column + size for _, _, size, column in ranges)
    n_k = max(k for k, _, _, _ in ranges) + 1
    half = jnp.bfloat16
    n_out = n_k * GROUP
    return pl.pallas_call(
        functools.partial(project_kernel, ranges, n_out),
        out_shape=[jax.ShapeDtypeStruct((rows, columns), half)] * n_out,
        in_specs=[pl.BlockSpec(memory_space=pltpu.SMEM)] + [whole] * (2 * GROUP + len(weights)),
        out_specs=[whole] * n_out,
        scratch_shapes=[
            pltpu.VMEM((rows, 2 * GROUP * width), half),
            pltpu.VMEM((GROUP, n_k, rows, columns), half),
        ],
        compiler_params=pltpu.CompilerParams(vmem_limit_bytes=40 * 2**20),
        cost_estimate=pl.CostEstimate(
            flops=4 * n_out * rows * columns * GROUP * width,
            bytes_accessed=8 * 2**20,
            transcendentals=0,
        ),
        name="project",
    )(pos, *inner, *edge, *weights)


def collect_kernel(sizes, pos, *refs):
    out = refs[-1]
    wide = out.shape[1] // 2
    x = pos[0]
    column = 0
    for b, size in enumerate(sizes):
        parts = refs[8 * b : 8 * b + 8]
        for a in range(2):
            total = None
            for n, part in enumerate(parts):
                if (n // 2) % 2 == a:
                    term = part[...].astype(jnp.float32)
                    total = term if total is None else total + term
            place = pl.multiple_of((x ^ a) * wide + column, BLOCK)
            out[:, pl.ds(place, size)] = total.astype(out.dtype)
        column += size


def collect(pos, batches):
    sizes = [batch[0].shape[1] for batch in batches]
    rows = batches[0][0].shape[0]
    whole = pl.BlockSpec(memory_space=pltpu.VMEM)
    return pl.pallas_call(
        functools.partial(collect_kernel, sizes),
        out_shape=jax.ShapeDtypeStruct((rows, 2 * sum(sizes)), jnp.bfloat16),
        in_specs=[pl.BlockSpec(memory_space=pltpu.SMEM)] + [whole] * (8 * len(sizes)),
        out_specs=whole,
        compiler_params=pltpu.CompilerParams(vmem_limit_bytes=16 * 2**20),
        name="collect",
    )(pos, *[part for batch in batches for part in batch])


def place_kernel(pos, *refs):
    out = refs[-1]
    for a, part in enumerate(refs[:-1]):
        rows, width = out.shape[0], part.shape[2]
        start = pl.multiple_of((pos[0] ^ a) * width, width)
        out[:, pl.ds(start, width)] = part[...].reshape(rows, width)


def place_columns(pos, parts):
    per_dev, block, width = parts[0].shape
    whole = pl.BlockSpec(memory_space=pltpu.VMEM)
    return pl.pallas_call(
        place_kernel,
        out_shape=jax.ShapeDtypeStruct((per_dev * block, GROUP * width), parts[0].dtype),
        in_specs=[pl.BlockSpec(memory_space=pltpu.SMEM)] + [whole] * len(parts),
        out_specs=whole,
        name="place_columns",
    )(pos, *parts)


def deliver(parts):
    arrived = []
    for n, part in enumerate(parts):
        a0, a1, a2 = n // 4, (n // 2) % 2, n % 2

        def route(t, s):
            g, z, x = t // GROUP, (t // 2) % 2, t % 2
            y, core = s // 2, s % 2
            return (g * GROUP + 2 * (core ^ a0) + (x ^ a1), 2 * (y ^ a2) + z)

        arrived.append(send(part, route))
    return arrived


def deliver_any(parts, group):
    groups = len(parts)
    secs = lax.axis_size("sec")
    rows, wide = parts[0].shape[1:]
    stacked = jnp.roll(jnp.stack(parts[::-1]), group + 1, axis=0)
    shape = (secs, groups // secs, GROUP, rows, wide)
    mine = lax.psum_scatter(stacked.reshape(shape), "sec", scatter_dimension=0, tiled=False)
    mine = jnp.moveaxis(mine, 1, 0)
    n_tgt = lax.axis_size("tgt")
    lists = [list(range(g, g + GROUP)) for g in range(0, n_tgt, GROUP)]
    mine = lax.all_to_all(mine, "tgt", 0, 0, axis_index_groups=lists)
    return jnp.transpose(mine, (2, 1, 0, 3)).reshape(rows, -1)


def after(block, *earlier):
    return lax.optimization_barrier((block, *earlier))[0]


def per_device(queries, key_values, grad_out, block_ids, block_count, kv_weight):
    rows_here, width_here = queries.shape
    blocks_here = rows_here // BLOCK
    width = width_here // GROUP
    n_tgt = lax.axis_size("tgt")
    groups = n_tgt // GROUP
    paired = groups == 2
    n_halo = 1 if paired else 2
    t, s = lax.axis_index("tgt"), lax.axis_index("sec")
    group, here = t // GROUP, t % GROUP
    start = jnp.where(group == 0, GROUP - 1, 0) if paired else 0

    def other_group(block):
        return send(block, lambda t, s: (t ^ GROUP, s))

    def shifted(block, k):
        return send(block, lambda t, s: (t + GROUP * k, s))

    wide = kv_weight.shape[1]
    if paired:
        cuts = [0, wide // 8, 3 * wide // 8, 3 * wide // 4, wide]
        chunks = [kv_weight[:, lo:hi] for lo, hi in zip(cuts, cuts[1:])]
        chunks[0] = other_group(chunks[0])

    total = (GROUP + n_halo) * blocks_here
    slots = (block_ids - group * GROUP * blocks_here) % total
    listed = jnp.concatenate([slots, block_count[:, None]], axis=1).astype(jnp.bfloat16)
    listed = jnp.pad(listed, ((0, 16 - blocks_here), (0, width - SLOTS - 1)))
    pairs, targets = [], []
    for a in range(GROUP):
        first = (here ^ a) * width
        pair = lax.dynamic_slice_in_dim(key_values, first, width, axis=2)
        pair = pair.reshape(2, blocks_here, BLOCK, width)
        pairs.append(pair if a == 0 else swap(pair, a))
    for a in range(GROUP):
        first = (here ^ a) * width
        target = jnp.concatenate(
            [lax.dynamic_slice_in_dim(part, first, width, axis=1) for part in (queries, grad_out)]
            + [listed]
        )
        targets.append(target if a == 0 else swap(target, a))
    def member(m):
        chosen = pairs[0]
        for a in range(1, GROUP):
            chosen = jnp.where(here ^ a == m, pairs[a], chosen)
        return chosen

    if paired:
        halos = [other_group(member(start))]
        chunks[1] = other_group(after(chunks[1], targets[1]))
    else:
        halos = [shifted(member(0), -1), shifted(member(GROUP - 1), 1)]

    meta = jnp.stack([target[2 * rows_here : 2 * rows_here + blocks_here, : SLOTS + 1] for target in targets])
    pos = jnp.stack([here, start]).astype(jnp.int32)
    dq, inner, edge, backs = attend(meta.astype(jnp.int32), pos, pairs, targets, halos)

    if paired:
        returned = other_group(backs[0])
        chunks[2] = other_group(after(chunks[2], returned))
    else:
        returned = jnp.concatenate([shifted(backs[1], -1), shifted(backs[0], 1)], axis=1)
    edge = (edge + returned.astype(jnp.float32)).astype(jnp.bfloat16)
    inners = [inner] + [swap(inner, a) for a in range(1, GROUP)]
    if paired:
        chunks[3] = other_group(after(chunks[3], inners[1]))
    edges = [edge] + [swap(edge, a) for a in range(1, GROUP)]

    core, y, x = s % 2, s // 2, t % 2
    if paired:
        order = [2 * (core ^ (j // 2)) + (x ^ (j % 2)) for j in range(GROUP)]
        pos = jnp.stack([here, start, y ^ group] + order).astype(jnp.int32)
        cut = cuts[3]
        ranges = [(0, 0, cut, 0)] + [(1, 0, hi - lo, lo) for lo, hi in zip(cuts[:3], cuts[1:4])]
        batch = deliver(project(pos, inners, edges, [kv_weight] + chunks[:3], ranges))
        ranges = [(0, cut, wide - cut, 0), (1, 0, wide - cut, 0)]
        last = deliver(project(pos, inners, edges, [kv_weight, chunks[3]], ranges))
        grad_memory = collect(x.astype(jnp.int32).reshape(1), [batch, last])
    else:
        pos = jnp.stack([here, start, 0] + list(range(GROUP))).astype(jnp.int32)
        weights = [kv_weight] + [
            send(kv_weight, lambda t, s, k=k: ((t + GROUP * k) % n_tgt, s))
            for k in range(1, groups)
        ]
        parts = [project(pos, inners, edges, [w], [(0, 0, wide, 0)]) for w in weights]
        grad_memory = deliver_any([jnp.stack(part) for part in parts], group)

    dq = [dq[0]] + [swap(dq[a], a) for a in range(1, GROUP)]
    return place_columns(here.astype(jnp.int32).reshape(1), dq), grad_memory


def solution(mesh):
    return jax.shard_map(
        per_device,
        mesh=mesh,
        in_specs=(
            P("tgt", "sec"),
            P(None, "tgt", "sec"),
            P("tgt", "sec"),
            P("tgt", None),
            P("tgt"),
            P(None, "tgt", "sec"),
        ),
        out_specs=(P("tgt", "sec"), P("tgt", "sec")),
        check_vma=False,
    )
```

```python
import functools
import math

import jax
import jax.numpy as jnp
from jax import lax
from jax.experimental import pallas as pl
from jax.experimental.pallas import tpu as pltpu
from jax.sharding import PartitionSpec as P

HEAD_DIM = 64
BLOCK = 128
SLOTS = 4
GROUP = 4
AXES = ("tgt", "sec")
SCALE = 0.125
NT = (((1,), (1,)), ((), ()))
TN = (((0,), (0,)), ((), ()))


def send(block, route):
    rows, secs = lax.axis_size("tgt"), lax.axis_size("sec")
    pairs = []
    for t in range(rows):
        for s in range(secs):
            target = route(t, s)
            if target is not None and 0 <= target[0] < rows:
                pairs.append((t * secs + s, target[0] * secs + target[1]))
    return lax.ppermute(block, AXES, pairs)


def swap(block, a):
    return send(block, lambda t, s: (t ^ a, s))


def pack_kernel(pos, queries, grad_out, key_values, listed, *outs):
    width = outs[0].shape[1]
    size = queries.shape[0]
    for a, out in enumerate(outs):
        columns = pl.ds(pl.multiple_of((pos[0] ^ a) * width, width), width)
        out[0:size] = queries[:, columns]
        out[size : 2 * size] = grad_out[:, columns]
        out[2 * size : 3 * size] = key_values[0, :, columns]
        out[3 * size : 4 * size] = key_values[1, :, columns]
        out[4 * size :] = listed[...]


def pack(pos, queries, grad_out, key_values, listed):
    width = listed.shape[1]
    shape = jax.ShapeDtypeStruct((4 * queries.shape[0] + listed.shape[0], width), queries.dtype)
    whole = pl.BlockSpec(memory_space=pltpu.VMEM)
    return pl.pallas_call(
        pack_kernel,
        out_shape=[shape] * GROUP,
        in_specs=[pl.BlockSpec(memory_space=pltpu.SMEM)] + [whole] * 4,
        out_specs=[whole] * GROUP,
        name="pack",
    )(pos, queries, grad_out, key_values, listed)


def attend_kernel(span, n_halo, with_halos, with_state, last, meta, pos, *refs):
    packs, refs = refs[:GROUP], refs[GROUP:]
    n_read = n_halo if with_halos else 0
    halos, refs = refs[:n_read], refs[n_read:]
    state, refs = refs[: 2 * with_state], refs[2 * with_state :]
    outs, (keys, values, rows, ups, kg, vg, qm, om) = refs[:-8], refs[-8:]
    acc, dq_all = outs[:2]
    own, width = dq_all.shape[0], dq_all.shape[2]
    per_dev = own // GROUP
    total = own + n_halo * per_dev
    size = per_dev * BLOCK
    heads = width // HEAD_DIM
    here, start = pos[0], pos[1]
    block = (per_dev, BLOCK, width)
    for a in range(GROUP):
        place = pl.ds((here ^ a) * per_dev, per_dev)
        for n, held in enumerate((rows, ups, keys, values)):
            held[place] = packs[a][n * size : (n + 1) * size].reshape(block)
    for n, halo in enumerate(halos):
        part = slice(own + n * per_dev, own + (n + 1) * per_dev)
        keys[part] = halo[:size].reshape(block)
        values[part] = halo[size:].reshape(block)
    if with_state:
        acc[...] = state[0][...]
        dq_all[...] = state[1][...]
    else:
        acc[...] = jnp.zeros_like(acc)
        dq_all[...] = jnp.zeros_like(dq_all)
    lane_head = lax.broadcasted_iota(jnp.int32, (BLOCK, width), 1) // HEAD_DIM
    key_row = lax.broadcasted_iota(jnp.int32, (SLOTS * BLOCK, heads * BLOCK), 0)

    def step(turn, carry):
        member = lax.rem(start + 1 + turn // per_dev, GROUP)
        a = here ^ member
        r = lax.rem(turn, per_dev)
        i = member * per_dev + r
        count = meta[a, r, SLOTS]
        ids = [jnp.clip(meta[a, r, s], 0, total - 1) for s in range(SLOTS)]
        for s in range(SLOTS):
            kg[s * BLOCK : (s + 1) * BLOCK] = keys[ids[s]]
            vg[s * BLOCK : (s + 1) * BLOCK] = values[ids[s]]
        q, o = rows[i], ups[i]
        for h in range(heads):
            qm[h * BLOCK : (h + 1) * BLOCK] = jnp.where(lane_head == h, q, 0)
            om[h * BLOCK : (h + 1) * BLOCK] = jnp.where(lane_head == h, o, 0)
        scores = lax.dot_general(kg[...], qm[...], NT, preferred_element_type=jnp.float32)
        scores = jnp.where(key_row < count * BLOCK, scores, -jnp.inf)
        top = jnp.max(scores, axis=0, keepdims=True)
        expo = jnp.exp2((scores - top) * (SCALE * math.log2(math.e)))
        probs = expo * (1.0 / jnp.sum(expo, axis=0, keepdims=True))
        probs_half = probs.astype(jnp.bfloat16)
        grad_probs = lax.dot_general(vg[...], om[...], NT, preferred_element_type=jnp.float32)
        delta = jnp.sum(probs_half.astype(jnp.float32) * grad_probs, axis=0, keepdims=True)
        grad_half = (probs * (grad_probs - delta)).astype(jnp.bfloat16)
        grad_value = jnp.dot(probs_half, om[...], preferred_element_type=jnp.float32)
        grad_key = SCALE * jnp.dot(grad_half, qm[...], preferred_element_type=jnp.float32)
        for s in range(SLOTS):
            part = slice(s * BLOCK, (s + 1) * BLOCK)
            acc[0, ids[s]] += grad_key[part]
            acc[1, ids[s]] += grad_value[part]
        flipped = lax.dot_general(kg[...], grad_half, TN, preferred_element_type=jnp.float32)
        flipped = jnp.concatenate(
            [
                flipped[h * HEAD_DIM : (h + 1) * HEAD_DIM, h * BLOCK : (h + 1) * BLOCK]
                for h in range(heads)
            ],
            axis=0,
        )
        dq_all[i] = (SCALE * flipped.T).astype(jnp.bfloat16)
        return carry

    lax.fori_loop(span[0], span[1], step, 0)
    half = jnp.bfloat16
    if last:
        dq_outs, (inner, edge) = outs[2 : 2 + GROUP], outs[2 + GROUP :]
        for a in range(GROUP):
            dq_outs[a][...] = dq_all[pl.ds((here ^ a) * per_dev, per_dev)]
        for p in range(GROUP):
            member = lax.rem(start + 1 + p, GROUP)
            taken = acc[:, pl.ds(member * per_dev, per_dev)]
            if p < GROUP - n_halo:
                inner[:, p * per_dev : (p + 1) * per_dev] = taken.astype(half)
            else:
                p -= GROUP - n_halo
                edge[:, p * per_dev : (p + 1) * per_dev] = taken
    elif with_halos:
        for n, back in enumerate(outs[2:]):
            part = slice(own + n * per_dev, own + (n + 1) * per_dev)
            back[...] = acc[:, part].astype(half)


def attend(span, n_halo, meta, pos, packs, halos=(), state=(), last=False):
    per_dev, width = meta.shape[1], packs[0].shape[1]
    own = GROUP * per_dev
    total = own + n_halo * per_dev
    heads = width // HEAD_DIM
    half = jnp.bfloat16
    block = (BLOCK, width)
    shapes = [
        jax.ShapeDtypeStruct((2, total) + block, jnp.float32),
        jax.ShapeDtypeStruct((own,) + block, half),
    ]
    if last:
        shapes += [jax.ShapeDtypeStruct((per_dev,) + block, half)] * GROUP
        shapes.append(jax.ShapeDtypeStruct((2, own - n_halo * per_dev) + block, half))
        shapes.append(jax.ShapeDtypeStruct((2, n_halo * per_dev) + block, jnp.float32))
    elif halos:
        shapes += [jax.ShapeDtypeStruct((2, per_dev) + block, half)] * n_halo
    scratch = (
        [pltpu.VMEM((total,) + block, half)] * 2
        + [pltpu.VMEM((own,) + block, half)] * 2
        + [pltpu.VMEM((SLOTS * BLOCK, width), half)] * 2
        + [pltpu.VMEM((heads * BLOCK, width), half)] * 2
    )
    whole = pl.BlockSpec(memory_space=pltpu.VMEM)
    scalars = pl.BlockSpec(memory_space=pltpu.SMEM)
    turns = span[1] - span[0]
    results = pl.pallas_call(
        functools.partial(attend_kernel, span, n_halo, bool(halos), bool(state), last),
        out_shape=shapes,
        in_specs=[scalars] * 2 + [whole] * (GROUP + len(halos) + len(state)),
        out_specs=[whole] * len(shapes),
        scratch_shapes=scratch,
        compiler_params=pltpu.CompilerParams(vmem_limit_bytes=20 * 2**20),
        cost_estimate=pl.CostEstimate(
            flops=turns * 10 * SLOTS * BLOCK * heads * BLOCK * width,
            bytes_accessed=4 * 2**20,
            transcendentals=turns * SLOTS * heads * BLOCK * BLOCK,
        ),
        name="attend",
    )(meta, pos, *packs, *halos, *state)
    return results[:2], results[2:]


def project_kernel(parts, pos, *refs):
    grads, sources, refs = refs[:GROUP], refs[GROUP : GROUP + len(parts)], refs[GROUP + len(parts) :]
    outs, (left, weights, sems) = refs[:-3], refs[-3:]
    width = grads[0].shape[1]
    rows = grads[0].shape[0] // (2 * GROUP)
    depth = GROUP * width
    per_out = outs[0].shape[0]
    here, start, in_middle = pos[0], pos[1], pos[2]

    def transfer(finish):
        for n, (source, (where, first, size, column)) in enumerate(zip(sources, parts)):

            def move():
                for c in range(2):
                    target = weights.at[c, pl.ds(column, size)]
                    sem = sems.at[n, c]
                    copy = pltpu.make_async_copy(source.at[c, pl.ds(first, size)], target, sem)
                    copy.wait() if finish else copy.start()

            if where is None:
                move()
            else:
                pl.when(in_middle == where)(move)

    transfer(False)
    for j in range(per_out * len(outs)):
        p = lax.rem(pos[3 + j] + (GROUP - 1) - start, GROUP)
        for a in range(GROUP):
            column = (here ^ a) * width
            for c in range(2):
                first = pl.multiple_of((c * GROUP + p) * rows, rows)
                piece = grads[a][pl.ds(first, rows)]
                place = pl.ds(pl.multiple_of(c * depth + column, width), width)
                left[j * rows : (j + 1) * rows, place] = piece
    transfer(True)
    total = None
    for c in range(2):
        term = lax.dot_general(
            left[:, c * depth : (c + 1) * depth],
            weights[c],
            NT,
            preferred_element_type=jnp.float32,
        )
        total = term if total is None else total + term
    total = total.astype(left.dtype)
    for n, out in enumerate(outs):
        for j in range(per_out):
            place = n * per_out + j
            out[j] = total[place * rows : (place + 1) * rows]


def project(pos, rows_at, n_out, grads, parts):
    rows = grads[0].shape[0] // (2 * GROUP)
    depth = GROUP * grads[0].shape[1]
    columns = max(column + size for _, (_, _, size, column) in parts)
    half = jnp.bfloat16
    whole = pl.BlockSpec(memory_space=pltpu.VMEM)
    anywhere = pl.BlockSpec(memory_space=pl.ANY)
    count = len(rows_at)
    pos = jnp.stack(list(pos) + list(rows_at)).astype(jnp.int32)
    return pl.pallas_call(
        functools.partial(project_kernel, [part for _, part in parts]),
        out_shape=[jax.ShapeDtypeStruct((count // n_out, rows, columns), half)] * n_out,
        in_specs=[pl.BlockSpec(memory_space=pltpu.SMEM)]
        + [whole] * GROUP
        + [anywhere] * len(parts),
        out_specs=[whole] * n_out,
        scratch_shapes=[
            pltpu.VMEM((count * rows, 2 * depth), half),
            pltpu.VMEM((2, columns, depth), half),
            pltpu.SemaphoreType.DMA((len(parts), 2)),
        ],
        compiler_params=pltpu.CompilerParams(vmem_limit_bytes=20 * 2**20),
        cost_estimate=pl.CostEstimate(
            flops=4 * count * rows * columns * depth,
            bytes_accessed=6 * 2**20,
            transcendentals=0,
        ),
        name="project",
    )(pos, *grads, *[weight for weight, _ in parts])


def merge_kernel(flip, kept_own, kept_other, given_own, given_other, *outs):
    sums = ((kept_own, given_own), (kept_other, given_other))
    for order in range(2):

        @pl.when(flip[0] == order)
        def _():
            for n, out in enumerate(outs):
                kept, given = sums[(n % 2) ^ order]
                total = kept[n // 2].astype(jnp.float32) + given[n // 2].astype(jnp.float32)
                out[...] = total.astype(out.dtype)


def merge(flip, *parts):
    whole = pl.BlockSpec(memory_space=pltpu.VMEM)
    n_out = 2 * parts[0].shape[0]
    return pl.pallas_call(
        merge_kernel,
        out_shape=[jax.ShapeDtypeStruct(parts[0].shape[1:], parts[0].dtype)] * n_out,
        in_specs=[pl.BlockSpec(memory_space=pltpu.SMEM)] + [whole] * 4,
        out_specs=[whole] * n_out,
        name="merge",
    )(flip, *parts)


def collect_kernel(pos, *refs):
    parts, out = refs[:-1], refs[-1]
    wide = out.shape[1] // 2
    for a in range(2):
        total = parts[2 * a][...].astype(jnp.float32) + parts[2 * a + 1][...].astype(jnp.float32)
        out[:, pl.ds(pl.multiple_of((pos[0] ^ a) * wide, wide), wide)] = total.astype(out.dtype)


def collect(pos, parts):
    rows, wide = parts[0].shape
    whole = pl.BlockSpec(memory_space=pltpu.VMEM)
    return pl.pallas_call(
        collect_kernel,
        out_shape=jax.ShapeDtypeStruct((rows, 2 * wide), parts[0].dtype),
        in_specs=[pl.BlockSpec(memory_space=pltpu.SMEM)] + [whole] * 4,
        out_specs=whole,
        name="collect",
    )(pos, *parts)


def place_kernel(starts, pos, *refs):
    parts, (out, held, sems) = refs[:GROUP], refs[GROUP:]
    rows, width = held.shape[1:]
    copies = [
        pltpu.make_async_copy(part.at[pl.ds(start, rows)], held.at[a], sems.at[a])
        for a, (part, start) in enumerate(zip(parts, starts))
    ]
    for copy in copies:
        copy.start()
    for a, copy in enumerate(copies):
        copy.wait()
        out[:, pl.ds(pl.multiple_of((pos[0] ^ a) * width, width), width)] = held[a]


def place_columns(pos, rows, parts, starts):
    width = parts[0].shape[1]
    half = parts[0].dtype
    anywhere = pl.BlockSpec(memory_space=pl.ANY)
    return pl.pallas_call(
        functools.partial(place_kernel, starts),
        out_shape=jax.ShapeDtypeStruct((rows, GROUP * width), half),
        in_specs=[pl.BlockSpec(memory_space=pltpu.SMEM)] + [anywhere] * GROUP,
        out_specs=pl.BlockSpec(memory_space=pltpu.VMEM),
        scratch_shapes=[pltpu.VMEM((GROUP, rows, width), half), pltpu.SemaphoreType.DMA((GROUP,))],
        name="place_columns",
    )(pos, *parts)


def other_core(block):
    return send(block, lambda t, s: (t, s ^ 1))


def deliver(parts):
    arrived = []
    for n, part in enumerate(parts):
        a1, a2 = n // 2, n % 2

        def route(t, s):
            g, z, x = t // GROUP, (t // 2) % 2, t % 2
            y, core = s // 2, s % 2
            return (g * GROUP + 2 * core + (x ^ a1), 2 * (y ^ a2) + (z ^ y ^ a2 ^ g))

        arrived.append(send(part, route))
    return arrived


def deliver_any(parts, group):
    groups = len(parts)
    secs = lax.axis_size("sec")
    rows, wide = parts[0].shape[1:]
    stacked = jnp.roll(jnp.stack(parts[::-1]), group + 1, axis=0)
    shape = (secs, groups // secs, GROUP, rows, wide)
    mine = lax.psum_scatter(stacked.reshape(shape), "sec", scatter_dimension=0, tiled=False)
    mine = jnp.moveaxis(mine, 1, 0)
    n_tgt = lax.axis_size("tgt")
    lists = [list(range(g, g + GROUP)) for g in range(0, n_tgt, GROUP)]
    mine = lax.all_to_all(mine, "tgt", 0, 0, axis_index_groups=lists)
    return jnp.transpose(mine, (2, 1, 0, 3)).reshape(rows, -1)


def after(block, *earlier):
    return lax.optimization_barrier((block, *earlier))[0]


def per_device(queries, key_values, grad_out, block_ids, block_count, kv_weight):
    rows_here, width_here = queries.shape
    blocks_here = rows_here // BLOCK
    width = width_here // GROUP
    n_tgt = lax.axis_size("tgt")
    groups = n_tgt // GROUP
    paired = groups == 2
    n_halo = 1 if paired else 2
    t, s = lax.axis_index("tgt"), lax.axis_index("sec")
    group, here = t // GROUP, t % GROUP
    start = jnp.where(group == 0, GROUP - 1, 0) if paired else 0
    pos = jnp.stack([here, start]).astype(jnp.int32)

    def other_group(block):
        return send(block, lambda t, s: (t ^ GROUP, s))

    def middle(block):
        return send(block, lambda t, s: (t ^ 6, s) if t // 2 in (1, 2) else None)

    def ends(block):
        return send(block, lambda t, s: (t ^ 6, s) if t // 2 in (0, 3) else None)

    def shifted(block, k):
        return send(block, lambda t, s: (t + GROUP * k, s))

    wide = kv_weight.shape[1]
    unit = wide // 16
    middle_cuts, end_cuts = (0, 8, 16), (0, 16)

    def rows_of(cuts, n):
        return kv_weight[:, cuts[n] * unit : cuts[n + 1] * unit]

    total = (GROUP + n_halo) * blocks_here
    slots = (block_ids - group * GROUP * blocks_here) % total
    listed = jnp.concatenate([slots, block_count[:, None]], axis=1).astype(jnp.bfloat16)
    listed = jnp.pad(listed, ((0, 16 - blocks_here), (0, width - SLOTS - 1)))
    packs = pack(pos, queries, grad_out, key_values, listed)
    if paired:
        middles = [middle(after(rows_of(middle_cuts, 0), packs[0]))]
    packs = [packs[0]] + [swap(packs[a], a) for a in range(1, GROUP)]
    pairs = [p[2 * rows_here : 4 * rows_here] for p in packs]

    def member(m):
        chosen = pairs[0]
        for a in range(1, GROUP):
            chosen = jnp.where(here ^ a == m, pairs[a], chosen)
        return chosen

    if paired:
        halos = [other_group(after(member(start), middles[0]))]
    else:
        halos = [shifted(member(0), -1), shifted(member(GROUP - 1), 1)]

    meta = jnp.stack([p[4 * rows_here : 4 * rows_here + blocks_here, : SLOTS + 1] for p in packs])
    meta = meta.astype(jnp.int32)
    own = GROUP * blocks_here
    n_inner = own - n_halo * blocks_here
    state, _ = attend((0, n_inner // 2), n_halo, meta, pos, packs)
    state, backs = attend((n_inner, own), n_halo, meta, pos, packs, halos, state)
    if paired:
        returned = other_group(backs[0])
    else:
        returned = jnp.concatenate([shifted(backs[1], -1), shifted(backs[0], 1)], axis=1)
    _, results = attend((n_inner // 2, n_inner), n_halo, meta, pos, packs, (), state, True)
    dq, (inner, edge) = results[:GROUP], results[GROUP:]
    edge = (edge + returned.astype(jnp.float32)).astype(jnp.bfloat16)
    grads = jnp.concatenate([inner, edge], axis=1).reshape(-1, width)
    dq = [block.reshape(rows_here, width) for block in dq]
    if paired:
        middles.append(middle(after(rows_of(middle_cuts, 1), returned)))
    near = swap(jnp.concatenate([grads, dq[1]]), 1)
    beside = swap(jnp.concatenate([grads, dq[2], dq[3]]), 2)
    if paired:
        far = [ends(after(rows_of(end_cuts, 0), beside, middles[1]))]
        beside = after(beside, near, middles[1])
    across = swap(beside, 1)
    done = grads.shape[0]
    dq = [dq[0], near, beside, across]
    starts = (0, done, done, done + rows_here)
    grads = [grads, near, beside, across]

    if paired:
        in_middle = ((t // 2 == 1) | (t // 2 == 2)).astype(jnp.int32)
        core, y, x = s % 2, s // 2, t % 2
        pos = [here, start, in_middle]
        order = [2 * z + (x ^ a) for z in (core ^ 1, core) for a in range(2)]
        give_own, keep_own = project(pos, order, 2, grads, [(kv_weight, (None, 0, wide, 0))])
        given_own = other_core(give_own)
        parts = []
        for where, weights, cuts in ((1, middles, middle_cuts), (0, far, end_cuts)):
            for weight, lo, hi in zip(weights, cuts, cuts[1:]):
                parts.append((weight, (where, 0, (hi - lo) * unit, lo * unit)))
        give_other, keep_other = project(pos, order, 2, grads, parts)
        given_other = other_core(give_other)
        flip = (y ^ group).astype(jnp.int32).reshape(1)
        arrived = deliver(merge(flip, keep_own, keep_other, given_own, given_other))
        grad_memory = collect(x.astype(jnp.int32).reshape(1), arrived)
    else:
        weights = [kv_weight] + [
            send(kv_weight, lambda t, s, k=k: ((t + GROUP * k) % n_tgt, s))
            for k in range(1, groups)
        ]
        pos, rows_at = [here, start, 0], list(range(GROUP))
        parts = [project(pos, rows_at, 1, grads, [(w, (None, 0, wide, 0))])[0] for w in weights]
        grad_memory = deliver_any(parts, group)

    here = here.astype(jnp.int32).reshape(1)
    return place_columns(here, rows_here, dq, starts), grad_memory


def solution(mesh):
    return jax.shard_map(
        per_device,
        mesh=mesh,
        in_specs=(
            P("tgt", "sec"),
            P(None, "tgt", "sec"),
            P("tgt", "sec"),
            P("tgt", None),
            P("tgt"),
            P(None, "tgt", "sec"),
        ),
        out_specs=(P("tgt", "sec"), P("tgt", "sec")),
        check_vma=False,
    )
```

```python
import functools
import math

import jax
import jax.numpy as jnp
from jax import lax
from jax.experimental import pallas as pl
from jax.experimental.pallas import tpu as pltpu
from jax.sharding import PartitionSpec as P

HEAD_DIM = 64
BLOCK = 128
SLOTS = 4
GROUP = 4
AXES = ("tgt", "sec")
SCALE = 0.125
NT = (((1,), (1,)), ((), ()))
TN = (((0,), (0,)), ((), ()))


def send(block, route):
    rows, secs = lax.axis_size("tgt"), lax.axis_size("sec")
    pairs = []
    for t in range(rows):
        for s in range(secs):
            target = route(t, s)
            if target is not None and 0 <= target[0] < rows:
                pairs.append((t * secs + s, target[0] * secs + target[1]))
    return lax.ppermute(block, AXES, pairs)


def swap(block, a):
    return send(block, lambda t, s: (t ^ a, s))


def pack_kernel(total, block_ids, block_count, queries, grad_out, key_values, *outs):
    width = outs[0].shape[1]
    size = queries.shape[0]
    position = lax.axis_index("tgt")
    here, group = lax.rem(position, GROUP), lax.div(position, GROUP)
    blocks_here, slots = block_ids.shape
    shape = (outs[0].shape[0] - 4 * size, width)
    row = lax.broadcasted_iota(jnp.int32, shape, 0)
    column = lax.broadcasted_iota(jnp.int32, shape, 1)
    lists = jnp.zeros(shape, jnp.int32)
    for r in range(blocks_here):
        for n in range(slots):
            slot = lax.rem(block_ids[r, n] - group * GROUP * blocks_here + total, total)
            lists = jnp.where((row == r) & (column == n), slot, lists)
        lists = jnp.where((row == r) & (column == slots), block_count[r], lists)
    lists = lists.astype(jnp.float32).astype(outs[0].dtype)
    for a, out in enumerate(outs):
        columns = pl.ds(pl.multiple_of((here ^ a) * width, width), width)
        out[0:size] = queries[:, columns]
        out[size : 2 * size] = grad_out[:, columns]
        out[2 * size : 3 * size] = key_values[0, :, columns]
        out[3 * size : 4 * size] = key_values[1, :, columns]
        out[4 * size :] = lists


def pack(total, block_ids, block_count, queries, grad_out, key_values):
    width = queries.shape[1] // GROUP
    shape = jax.ShapeDtypeStruct((4 * queries.shape[0] + 16, width), queries.dtype)
    whole = pl.BlockSpec(memory_space=pltpu.VMEM)
    scalars = pl.BlockSpec(memory_space=pltpu.SMEM)
    return pl.pallas_call(
        functools.partial(pack_kernel, total),
        out_shape=[shape] * GROUP,
        in_specs=[scalars] * 2 + [whole] * 3,
        out_specs=[whole] * GROUP,
        name="pack",
    )(block_ids, block_count, queries, grad_out, key_values)


def attend_kernel(span, n_halo, with_halos, with_state, last, meta, pos, *refs):
    packs, refs = refs[:GROUP], refs[GROUP:]
    n_read = n_halo if with_halos else 0
    halos, refs = refs[:n_read], refs[n_read:]
    state, refs = refs[: 2 * with_state], refs[2 * with_state :]
    outs, (keys, values, rows, ups, kg, vg, qm, om) = refs[:-8], refs[-8:]
    acc, dq_all = outs[:2]
    own, width = dq_all.shape[0], dq_all.shape[2]
    per_dev = own // GROUP
    total = own + n_halo * per_dev
    size = per_dev * BLOCK
    heads = width // HEAD_DIM
    here, start = pos[0], pos[1]
    block = (per_dev, BLOCK, width)
    for a in range(GROUP):
        place = pl.ds((here ^ a) * per_dev, per_dev)
        for n, held in enumerate((rows, ups, keys, values)):
            held[place] = packs[a][n * size : (n + 1) * size].reshape(block)
    for n, halo in enumerate(halos):
        part = slice(own + n * per_dev, own + (n + 1) * per_dev)
        keys[part] = halo[:size].reshape(block)
        values[part] = halo[size:].reshape(block)
    if with_state:
        acc[...] = state[0][...]
        dq_all[...] = state[1][...]
    else:
        acc[...] = jnp.zeros_like(acc)
        dq_all[...] = jnp.zeros_like(dq_all)
    lane_head = lax.broadcasted_iota(jnp.int32, (BLOCK, width), 1) // HEAD_DIM
    key_row = lax.broadcasted_iota(jnp.int32, (SLOTS * BLOCK, heads * BLOCK), 0)

    def step(turn, carry):
        member = lax.rem(start + 1 + turn // per_dev, GROUP)
        a = here ^ member
        r = lax.rem(turn, per_dev)
        i = member * per_dev + r
        count = meta[a, r, SLOTS]
        ids = [jnp.clip(meta[a, r, s], 0, total - 1) for s in range(SLOTS)]
        for s in range(SLOTS):
            kg[s * BLOCK : (s + 1) * BLOCK] = keys[ids[s]]
            vg[s * BLOCK : (s + 1) * BLOCK] = values[ids[s]]
        q, o = rows[i], ups[i]
        for h in range(heads):
            qm[h * BLOCK : (h + 1) * BLOCK] = jnp.where(lane_head == h, q, 0)
            om[h * BLOCK : (h + 1) * BLOCK] = jnp.where(lane_head == h, o, 0)
        scores = lax.dot_general(kg[...], qm[...], NT, preferred_element_type=jnp.float32)
        scores = jnp.where(key_row < count * BLOCK, scores, -jnp.inf)
        top = jnp.max(scores, axis=0, keepdims=True)
        expo = jnp.exp2((scores - top) * (SCALE * math.log2(math.e)))
        probs = expo * (1.0 / jnp.sum(expo, axis=0, keepdims=True))
        probs_half = probs.astype(jnp.bfloat16)
        grad_probs = lax.dot_general(vg[...], om[...], NT, preferred_element_type=jnp.float32)
        delta = jnp.sum(probs_half.astype(jnp.float32) * grad_probs, axis=0, keepdims=True)
        grad_half = (probs * (grad_probs - delta)).astype(jnp.bfloat16)
        grad_value = jnp.dot(probs_half, om[...], preferred_element_type=jnp.float32)
        grad_key = SCALE * jnp.dot(grad_half, qm[...], preferred_element_type=jnp.float32)
        for s in range(SLOTS):
            part = slice(s * BLOCK, (s + 1) * BLOCK)
            acc[0, ids[s]] += grad_key[part]
            acc[1, ids[s]] += grad_value[part]
        flipped = lax.dot_general(kg[...], grad_half, TN, preferred_element_type=jnp.float32)
        flipped = jnp.concatenate(
            [
                flipped[h * HEAD_DIM : (h + 1) * HEAD_DIM, h * BLOCK : (h + 1) * BLOCK]
                for h in range(heads)
            ],
            axis=0,
        )
        dq_all[i] = (SCALE * flipped.T).astype(jnp.bfloat16)
        return carry

    lax.fori_loop(span[0], span[1], step, 0)
    half = jnp.bfloat16
    if last:
        dq_outs, (inner, edge) = outs[2 : 2 + GROUP], outs[2 + GROUP :]
        for a in range(GROUP):
            dq_outs[a][...] = dq_all[pl.ds((here ^ a) * per_dev, per_dev)]
        for p in range(GROUP):
            member = lax.rem(start + 1 + p, GROUP)
            taken = acc[:, pl.ds(member * per_dev, per_dev)]
            if p < GROUP - n_halo:
                inner[:, p * per_dev : (p + 1) * per_dev] = taken.astype(half)
            else:
                p -= GROUP - n_halo
                edge[:, p * per_dev : (p + 1) * per_dev] = taken
    elif with_halos:
        for n, back in enumerate(outs[2:]):
            part = slice(own + n * per_dev, own + (n + 1) * per_dev)
            back[...] = acc[:, part].astype(half)


def attend(span, n_halo, meta, pos, packs, halos=(), state=(), last=False):
    per_dev, width = meta.shape[1], packs[0].shape[1]
    own = GROUP * per_dev
    total = own + n_halo * per_dev
    heads = width // HEAD_DIM
    half = jnp.bfloat16
    block = (BLOCK, width)
    shapes = [
        jax.ShapeDtypeStruct((2, total) + block, jnp.float32),
        jax.ShapeDtypeStruct((own,) + block, half),
    ]
    if last:
        shapes += [jax.ShapeDtypeStruct((per_dev,) + block, half)] * GROUP
        shapes.append(jax.ShapeDtypeStruct((2, own - n_halo * per_dev) + block, half))
        shapes.append(jax.ShapeDtypeStruct((2, n_halo * per_dev) + block, jnp.float32))
    elif halos:
        shapes += [jax.ShapeDtypeStruct((2, per_dev) + block, half)] * n_halo
    scratch = (
        [pltpu.VMEM((total,) + block, half)] * 2
        + [pltpu.VMEM((own,) + block, half)] * 2
        + [pltpu.VMEM((SLOTS * BLOCK, width), half)] * 2
        + [pltpu.VMEM((heads * BLOCK, width), half)] * 2
    )
    whole = pl.BlockSpec(memory_space=pltpu.VMEM)
    scalars = pl.BlockSpec(memory_space=pltpu.SMEM)
    turns = span[1] - span[0]
    results = pl.pallas_call(
        functools.partial(attend_kernel, span, n_halo, bool(halos), bool(state), last),
        out_shape=shapes,
        in_specs=[scalars] * 2 + [whole] * (GROUP + len(halos) + len(state)),
        out_specs=[whole] * len(shapes),
        scratch_shapes=scratch,
        compiler_params=pltpu.CompilerParams(vmem_limit_bytes=20 * 2**20),
        cost_estimate=pl.CostEstimate(
            flops=turns * 10 * SLOTS * BLOCK * heads * BLOCK * width,
            bytes_accessed=4 * 2**20,
            transcendentals=turns * SLOTS * heads * BLOCK * BLOCK,
        ),
        name="attend",
    )(meta, pos, *packs, *halos, *state)
    return results[:2], results[2:]


def project_kernel(parts, pos, *refs):
    grads, sources, refs = refs[:GROUP], refs[GROUP : GROUP + len(parts)], refs[GROUP + len(parts) :]
    outs, (left, weights, sems) = refs[:-3], refs[-3:]
    width = grads[0].shape[1]
    rows = grads[0].shape[0] // (2 * GROUP)
    depth = GROUP * width
    per_out = outs[0].shape[0]
    here, start, in_middle = pos[0], pos[1], pos[2]

    def transfer(finish):
        for n, (source, (where, first, size, column)) in enumerate(zip(sources, parts)):

            def move():
                for c in range(2):
                    target = weights.at[c, pl.ds(column, size)]
                    sem = sems.at[n, c]
                    copy = pltpu.make_async_copy(source.at[c, pl.ds(first, size)], target, sem)
                    copy.wait() if finish else copy.start()

            if where is None:
                move()
            else:
                pl.when(in_middle == where)(move)

    transfer(False)
    for j in range(per_out * len(outs)):
        p = lax.rem(pos[3 + j] + (GROUP - 1) - start, GROUP)
        for a in range(GROUP):
            column = (here ^ a) * width
            for c in range(2):
                first = pl.multiple_of((c * GROUP + p) * rows, rows)
                piece = grads[a][pl.ds(first, rows)]
                place = pl.ds(pl.multiple_of(c * depth + column, width), width)
                left[j * rows : (j + 1) * rows, place] = piece
    transfer(True)
    total = None
    for c in range(2):
        term = lax.dot_general(
            left[:, c * depth : (c + 1) * depth],
            weights[c],
            NT,
            preferred_element_type=jnp.float32,
        )
        total = term if total is None else total + term
    total = total.astype(left.dtype)
    for n, out in enumerate(outs):
        for j in range(per_out):
            place = n * per_out + j
            out[j] = total[place * rows : (place + 1) * rows]


def project(pos, rows_at, n_out, grads, parts):
    rows = grads[0].shape[0] // (2 * GROUP)
    depth = GROUP * grads[0].shape[1]
    columns = max(column + size for _, (_, _, size, column) in parts)
    half = jnp.bfloat16
    whole = pl.BlockSpec(memory_space=pltpu.VMEM)
    anywhere = pl.BlockSpec(memory_space=pl.ANY)
    count = len(rows_at)
    pos = jnp.stack(list(pos) + list(rows_at)).astype(jnp.int32)
    return pl.pallas_call(
        functools.partial(project_kernel, [part for _, part in parts]),
        out_shape=[jax.ShapeDtypeStruct((count // n_out, rows, columns), half)] * n_out,
        in_specs=[pl.BlockSpec(memory_space=pltpu.SMEM)]
        + [whole] * GROUP
        + [anywhere] * len(parts),
        out_specs=[whole] * n_out,
        scratch_shapes=[
            pltpu.VMEM((count * rows, 2 * depth), half),
            pltpu.VMEM((2, columns, depth), half),
            pltpu.SemaphoreType.DMA((len(parts), 2)),
        ],
        compiler_params=pltpu.CompilerParams(vmem_limit_bytes=20 * 2**20),
        cost_estimate=pl.CostEstimate(
            flops=4 * count * rows * columns * depth,
            bytes_accessed=6 * 2**20,
            transcendentals=0,
        ),
        name="project",
    )(pos, *grads, *[weight for weight, _ in parts])


def merge_kernel(flip, *refs):
    kept_own, given_own = refs[:2]
    n_parts = (len(refs) - 2 - 4) // 2
    kept, given, outs = refs[2 : 2 + n_parts], refs[2 + n_parts : 2 + 2 * n_parts], refs[-4:]
    for order in range(2):

        @pl.when(flip[0] == order)
        def _():
            for n, out in enumerate(outs):
                if (n % 2) ^ order == 0:
                    terms = [(kept_own, given_own)]
                else:
                    terms = list(zip(kept, given))
                column = 0
                for left, right in terms:
                    size = left.shape[2]
                    total = left[n // 2].astype(jnp.float32) + right[n // 2].astype(jnp.float32)
                    out[:, column : column + size] = total.astype(out.dtype)
                    column += size


def merge(flip, kept_own, given_own, kept, given):
    whole = pl.BlockSpec(memory_space=pltpu.VMEM)
    return pl.pallas_call(
        merge_kernel,
        out_shape=[jax.ShapeDtypeStruct(kept_own.shape[1:], kept_own.dtype)] * 4,
        in_specs=[pl.BlockSpec(memory_space=pltpu.SMEM)] + [whole] * (2 + 2 * len(kept)),
        out_specs=[whole] * 4,
        name="merge",
    )(flip, kept_own, given_own, *kept, *given)


def collect_kernel(pos, *refs):
    parts, out = refs[:-1], refs[-1]
    wide = out.shape[1] // 2
    for a in range(2):
        total = parts[2 * a][...].astype(jnp.float32) + parts[2 * a + 1][...].astype(jnp.float32)
        out[:, pl.ds(pl.multiple_of((pos[0] ^ a) * wide, wide), wide)] = total.astype(out.dtype)


def collect(pos, parts):
    rows, wide = parts[0].shape
    whole = pl.BlockSpec(memory_space=pltpu.VMEM)
    return pl.pallas_call(
        collect_kernel,
        out_shape=jax.ShapeDtypeStruct((rows, 2 * wide), parts[0].dtype),
        in_specs=[pl.BlockSpec(memory_space=pltpu.SMEM)] + [whole] * 4,
        out_specs=whole,
        name="collect",
    )(pos, *parts)


def place_kernel(pos, *refs):
    out = refs[-1]
    for a, part in enumerate(refs[:-1]):
        width = part.shape[1]
        start = pl.multiple_of((pos[0] ^ a) * width, width)
        out[:, pl.ds(start, width)] = part[...]


def place_columns(pos, parts):
    rows, width = parts[0].shape
    whole = pl.BlockSpec(memory_space=pltpu.VMEM)
    return pl.pallas_call(
        place_kernel,
        out_shape=jax.ShapeDtypeStruct((rows, GROUP * width), parts[0].dtype),
        in_specs=[pl.BlockSpec(memory_space=pltpu.SMEM)] + [whole] * len(parts),
        out_specs=whole,
        name="place_columns",
    )(pos, *parts)


def other_core(block):
    return send(block, lambda t, s: (t, s ^ 1))


def deliver(parts):
    arrived = []
    for n, part in enumerate(parts):
        a1, a2 = n // 2, n % 2

        def route(t, s):
            g, z, x = t // GROUP, (t // 2) % 2, t % 2
            y, core = s // 2, s % 2
            return (g * GROUP + 2 * core + (x ^ a1), 2 * (y ^ a2) + (z ^ y ^ a2 ^ g))

        arrived.append(send(part, route))
    return arrived


def deliver_any(parts, group):
    groups = len(parts)
    secs = lax.axis_size("sec")
    rows, wide = parts[0].shape[1:]
    stacked = jnp.roll(jnp.stack(parts[::-1]), group + 1, axis=0)
    shape = (secs, groups // secs, GROUP, rows, wide)
    mine = lax.psum_scatter(stacked.reshape(shape), "sec", scatter_dimension=0, tiled=False)
    mine = jnp.moveaxis(mine, 1, 0)
    n_tgt = lax.axis_size("tgt")
    lists = [list(range(g, g + GROUP)) for g in range(0, n_tgt, GROUP)]
    mine = lax.all_to_all(mine, "tgt", 0, 0, axis_index_groups=lists)
    return jnp.transpose(mine, (2, 1, 0, 3)).reshape(rows, -1)


def after(block, *earlier):
    return lax.optimization_barrier((block, *earlier))[0]


def per_device(queries, key_values, grad_out, block_ids, block_count, kv_weight):
    rows_here, width_here = queries.shape
    blocks_here = rows_here // BLOCK
    width = width_here // GROUP
    n_tgt = lax.axis_size("tgt")
    groups = n_tgt // GROUP
    paired = groups == 2
    n_halo = 1 if paired else 2
    t, s = lax.axis_index("tgt"), lax.axis_index("sec")
    group, here = t // GROUP, t % GROUP
    start = jnp.where(group == 0, GROUP - 1, 0) if paired else 0
    pos = jnp.stack([here, start]).astype(jnp.int32)

    def other_group(block):
        return send(block, lambda t, s: (t ^ GROUP, s))

    def middle(block):
        return send(block, lambda t, s: (t ^ 6, s) if t // 2 in (1, 2) else None)

    def ends(block):
        return send(block, lambda t, s: (t ^ 6, s) if t // 2 in (0, 3) else None)

    def shifted(block, k):
        return send(block, lambda t, s: (t + GROUP * k, s))

    wide = kv_weight.shape[1]
    unit = wide // 16
    middle_cuts, end_cuts = (0, 8, 16), (0, 12, 16)

    def rows_of(cuts, n):
        return kv_weight[:, cuts[n] * unit : cuts[n + 1] * unit]

    total = (GROUP + n_halo) * blocks_here
    packs = pack(total, block_ids, block_count, queries, grad_out, key_values)
    if paired:
        middles = [middle(after(rows_of(middle_cuts, 0), packs[0]))]
    packs = [packs[0]] + [swap(packs[a], a) for a in range(1, GROUP)]
    pairs = [p[2 * rows_here : 4 * rows_here] for p in packs]

    def member(m):
        chosen = pairs[0]
        for a in range(1, GROUP):
            chosen = jnp.where(here ^ a == m, pairs[a], chosen)
        return chosen

    if paired:
        halos = [other_group(after(member(start), middles[0]))]
    else:
        halos = [shifted(member(0), -1), shifted(member(GROUP - 1), 1)]

    meta = jnp.stack([p[4 * rows_here : 4 * rows_here + blocks_here, : SLOTS + 1] for p in packs])
    meta = meta.astype(jnp.int32)
    own = GROUP * blocks_here
    n_inner = own - n_halo * blocks_here
    state, _ = attend((0, n_inner // 2), n_halo, meta, pos, packs)
    state, backs = attend((n_inner, own), n_halo, meta, pos, packs, halos, state)
    if paired:
        returned = other_group(backs[0])
    else:
        returned = jnp.concatenate([shifted(backs[1], -1), shifted(backs[0], 1)], axis=1)
    _, results = attend((n_inner // 2, n_inner), n_halo, meta, pos, packs, (), state, True)
    dq, (inner, edge) = results[:GROUP], results[GROUP:]
    edge = (edge + returned.astype(jnp.float32)).astype(jnp.bfloat16)
    grads = jnp.concatenate([inner, edge], axis=1).reshape(-1, width)
    dq = [block.reshape(rows_here, width) for block in dq]
    if paired:
        middles.append(middle(after(rows_of(middle_cuts, 1), returned)))
    near, beside = swap(grads, 1), swap(grads, 2)
    if paired:
        far = [ends(after(rows_of(end_cuts, 0), beside, middles[1]))]
        beside = after(beside, near, middles[1])
    grads = [grads, near, beside, swap(beside, 1)]
    dq = [dq[0]] + [swap(after(dq[a], grads[3]), a) for a in range(1, GROUP)]

    if paired:
        in_middle = ((t // 2 == 1) | (t // 2 == 2)).astype(jnp.int32)
        core, y, x = s % 2, s // 2, t % 2
        pos = [here, start, in_middle]
        order = [2 * z + (x ^ a) for z in (core ^ 1, core) for a in range(2)]
        give_own, keep_own = project(pos, order, 2, grads, [(kv_weight, (None, 0, wide, 0))])
        given_own = other_core(give_own)
        far.append(ends(after(rows_of(end_cuts, 1), grads[3])))
        kept, given = [], []
        for lo, hi in zip(end_cuts, end_cuts[1:]):
            parts = []
            for where, weights, cuts in ((1, middles, middle_cuts), (0, far, end_cuts)):
                for weight, first, last in zip(weights, cuts, cuts[1:]):
                    begin, end = max(first, lo), min(last, hi)
                    if begin < end:
                        span = ((begin - first) * unit, (end - begin) * unit, (begin - lo) * unit)
                        parts.append((weight, (where,) + span))
            give_other, keep_other = project(pos, order, 2, grads, parts)
            kept.append(keep_other)
            given.append(other_core(give_other))
        kept[-1] = after(kept[-1], *dq[1:])
        flip = (y ^ group).astype(jnp.int32).reshape(1)
        arrived = deliver(merge(flip, keep_own, given_own, kept, given))
        grad_memory = collect(x.astype(jnp.int32).reshape(1), arrived)
    else:
        weights = [kv_weight] + [
            send(kv_weight, lambda t, s, k=k: ((t + GROUP * k) % n_tgt, s))
            for k in range(1, groups)
        ]
        pos, rows_at = [here, start, 0], list(range(GROUP))
        parts = [project(pos, rows_at, 1, grads, [(w, (None, 0, wide, 0))])[0] for w in weights]
        grad_memory = deliver_any(parts, group)

    here = here.astype(jnp.int32).reshape(1)
    return place_columns(here, dq), grad_memory


def solution(mesh):
    return jax.shard_map(
        per_device,
        mesh=mesh,
        in_specs=(
            P("tgt", "sec"),
            P(None, "tgt", "sec"),
            P("tgt", "sec"),
            P("tgt", None),
            P("tgt"),
            P(None, "tgt", "sec"),
        ),
        out_specs=(P("tgt", "sec"), P("tgt", "sec")),
        check_vma=False,
    )
```

```python
import functools
import math

import jax
import jax.numpy as jnp
from jax import lax
from jax.experimental import pallas as pl
from jax.experimental.pallas import tpu as pltpu
from jax.sharding import PartitionSpec as P

HEAD_DIM = 64
BLOCK = 128
SLOTS = 4
GROUP = 4
AXES = ("tgt", "sec")
SCALE = 0.125
NT = (((1,), (1,)), ((), ()))
TN = (((0,), (0,)), ((), ()))


def send(block, route):
    rows, secs = lax.axis_size("tgt"), lax.axis_size("sec")
    pairs = []
    for t in range(rows):
        for s in range(secs):
            target = route(t, s)
            if target is not None and 0 <= target[0] < rows:
                pairs.append((t * secs + s, target[0] * secs + target[1]))
    return lax.ppermute(block, AXES, pairs)


def swap(block, a):
    return send(block, lambda t, s: (t ^ a, s))


def pack_kernel(total, block_ids, block_count, queries, grad_out, key_values, *outs):
    width = outs[0].shape[1]
    size = queries.shape[0]
    position = lax.axis_index("tgt")
    here, group = lax.rem(position, GROUP), lax.div(position, GROUP)
    blocks_here, slots = block_ids.shape
    shape = (outs[0].shape[0] - 4 * size, width)
    row = lax.broadcasted_iota(jnp.int32, shape, 0)
    column = lax.broadcasted_iota(jnp.int32, shape, 1)
    lists = jnp.zeros(shape, jnp.int32)
    for r in range(blocks_here):
        for n in range(slots):
            slot = lax.rem(block_ids[r, n] - group * GROUP * blocks_here + total, total)
            lists = jnp.where((row == r) & (column == n), slot, lists)
        lists = jnp.where((row == r) & (column == slots), block_count[r], lists)
    lists = lists.astype(jnp.float32).astype(outs[0].dtype)
    for a, out in enumerate(outs):
        columns = pl.ds(pl.multiple_of((here ^ a) * width, width), width)
        out[0:size] = queries[:, columns]
        out[size : 2 * size] = grad_out[:, columns]
        out[2 * size : 3 * size] = key_values[0, :, columns]
        out[3 * size : 4 * size] = key_values[1, :, columns]
        out[4 * size :] = lists


def pack(total, block_ids, block_count, queries, grad_out, key_values):
    width = queries.shape[1] // GROUP
    shape = jax.ShapeDtypeStruct((4 * queries.shape[0] + 16, width), queries.dtype)
    whole = pl.BlockSpec(memory_space=pltpu.VMEM)
    scalars = pl.BlockSpec(memory_space=pltpu.SMEM)
    return pl.pallas_call(
        functools.partial(pack_kernel, total),
        out_shape=[shape] * GROUP,
        in_specs=[scalars] * 2 + [whole] * 3,
        out_specs=[whole] * GROUP,
        name="pack",
    )(block_ids, block_count, queries, grad_out, key_values)


def attend_kernel(span, n_halo, with_halos, with_state, last, meta, pos, *refs):
    packs, refs = refs[:GROUP], refs[GROUP:]
    n_read = n_halo if with_halos else 0
    halos, refs = refs[:n_read], refs[n_read:]
    state, refs = refs[: 2 * with_state], refs[2 * with_state :]
    outs, (keys, values, rows, ups, kg, vg, qm, om) = refs[:-8], refs[-8:]
    acc, dq_all = outs[:2]
    own, width = dq_all.shape[0], dq_all.shape[2]
    per_dev = own // GROUP
    total = own + n_halo * per_dev
    size = per_dev * BLOCK
    heads = width // HEAD_DIM
    here, start = pos[0], pos[1]
    block = (per_dev, BLOCK, width)
    for a in range(GROUP):
        place = pl.ds((here ^ a) * per_dev, per_dev)
        for n, held in enumerate((rows, ups, keys, values)):
            held[place] = packs[a][n * size : (n + 1) * size].reshape(block)
    for n, halo in enumerate(halos):
        part = slice(own + n * per_dev, own + (n + 1) * per_dev)
        keys[part] = halo[:size].reshape(block)
        values[part] = halo[size:].reshape(block)
    if not with_state:
        acc[...] = jnp.zeros_like(acc)
        dq_all[...] = jnp.zeros_like(dq_all)
    lane_head = lax.broadcasted_iota(jnp.int32, (BLOCK, width), 1) // HEAD_DIM
    key_row = lax.broadcasted_iota(jnp.int32, (SLOTS * BLOCK, heads * BLOCK), 0)

    def step(turn, carry):
        member = lax.rem(start + 1 + turn // per_dev, GROUP)
        a = here ^ member
        r = lax.rem(turn, per_dev)
        i = member * per_dev + r
        count = meta[a, r, SLOTS]
        ids = [jnp.clip(meta[a, r, s], 0, total - 1) for s in range(SLOTS)]
        for s in range(SLOTS):
            kg[s * BLOCK : (s + 1) * BLOCK] = keys[ids[s]]
            vg[s * BLOCK : (s + 1) * BLOCK] = values[ids[s]]
        q, o = rows[i], ups[i]
        for h in range(heads):
            qm[h * BLOCK : (h + 1) * BLOCK] = jnp.where(lane_head == h, q, 0)
            om[h * BLOCK : (h + 1) * BLOCK] = jnp.where(lane_head == h, o, 0)
        scores = lax.dot_general(kg[...], qm[...], NT, preferred_element_type=jnp.float32)
        scores = jnp.where(key_row < count * BLOCK, scores, -jnp.inf)
        top = jnp.max(scores, axis=0, keepdims=True)
        expo = jnp.exp2((scores - top) * (SCALE * math.log2(math.e)))
        probs = expo * (1.0 / jnp.sum(expo, axis=0, keepdims=True))
        probs_half = probs.astype(jnp.bfloat16)
        grad_probs = lax.dot_general(vg[...], om[...], NT, preferred_element_type=jnp.float32)
        delta = jnp.sum(probs_half.astype(jnp.float32) * grad_probs, axis=0, keepdims=True)
        grad_half = (probs * (grad_probs - delta)).astype(jnp.bfloat16)
        grad_value = jnp.dot(probs_half, om[...], preferred_element_type=jnp.float32)
        grad_key = SCALE * jnp.dot(grad_half, qm[...], preferred_element_type=jnp.float32)
        for s in range(SLOTS):
            part = slice(s * BLOCK, (s + 1) * BLOCK)
            acc[0, ids[s]] += grad_key[part]
            acc[1, ids[s]] += grad_value[part]
        flipped = lax.dot_general(kg[...], grad_half, TN, preferred_element_type=jnp.float32)
        flipped = jnp.concatenate(
            [
                flipped[h * HEAD_DIM : (h + 1) * HEAD_DIM, h * BLOCK : (h + 1) * BLOCK]
                for h in range(heads)
            ],
            axis=0,
        )
        dq_all[i] = (SCALE * flipped.T).astype(jnp.bfloat16)
        return carry

    lax.fori_loop(span[0], span[1], step, 0)
    half = jnp.bfloat16
    if last:
        dq_outs, (inner, edge) = outs[2 : 2 + GROUP], outs[2 + GROUP :]
        for a in range(GROUP):
            dq_outs[a][...] = dq_all[pl.ds((here ^ a) * per_dev, per_dev)]
        for p in range(GROUP):
            member = lax.rem(start + 1 + p, GROUP)
            taken = acc[:, pl.ds(member * per_dev, per_dev)]
            if p < GROUP - n_halo:
                inner[:, p * per_dev : (p + 1) * per_dev] = taken.astype(half)
            else:
                p -= GROUP - n_halo
                edge[:, p * per_dev : (p + 1) * per_dev] = taken
    elif with_halos:
        for n, back in enumerate(outs[2:]):
            part = slice(own + n * per_dev, own + (n + 1) * per_dev)
            back[...] = acc[:, part].astype(half)


def attend(span, n_halo, meta, pos, packs, halos=(), state=(), last=False):
    per_dev, width = meta.shape[1], packs[0].shape[1]
    own = GROUP * per_dev
    total = own + n_halo * per_dev
    heads = width // HEAD_DIM
    half = jnp.bfloat16
    block = (BLOCK, width)
    shapes = [
        jax.ShapeDtypeStruct((2, total) + block, jnp.float32),
        jax.ShapeDtypeStruct((own,) + block, half),
    ]
    if last:
        shapes += [jax.ShapeDtypeStruct((per_dev,) + block, half)] * GROUP
        shapes.append(jax.ShapeDtypeStruct((2, own - n_halo * per_dev) + block, half))
        shapes.append(jax.ShapeDtypeStruct((2, n_halo * per_dev) + block, jnp.float32))
    elif halos:
        shapes += [jax.ShapeDtypeStruct((2, per_dev) + block, half)] * n_halo
    scratch = (
        [pltpu.VMEM((total,) + block, half)] * 2
        + [pltpu.VMEM((own,) + block, half)] * 2
        + [pltpu.VMEM((SLOTS * BLOCK, width), half)] * 2
        + [pltpu.VMEM((heads * BLOCK, width), half)] * 2
    )
    whole = pl.BlockSpec(memory_space=pltpu.VMEM)
    scalars = pl.BlockSpec(memory_space=pltpu.SMEM)
    turns = span[1] - span[0]
    results = pl.pallas_call(
        functools.partial(attend_kernel, span, n_halo, bool(halos), bool(state), last),
        out_shape=shapes,
        in_specs=[scalars] * 2 + [whole] * (GROUP + len(halos) + len(state)),
        out_specs=[whole] * len(shapes),
        scratch_shapes=scratch,
        input_output_aliases={2 + GROUP + len(halos) + n: n for n in range(len(state))},
        compiler_params=pltpu.CompilerParams(vmem_limit_bytes=20 * 2**20),
        cost_estimate=pl.CostEstimate(
            flops=turns * 10 * SLOTS * BLOCK * heads * BLOCK * width,
            bytes_accessed=4 * 2**20,
            transcendentals=turns * SLOTS * heads * BLOCK * BLOCK,
        ),
        name="attend",
    )(meta, pos, *packs, *halos, *state)
    return results[:2], results[2:]


def project_kernel(parts, pos, *refs):
    grads, sources, refs = refs[:GROUP], refs[GROUP : GROUP + len(parts)], refs[GROUP + len(parts) :]
    outs, (total, weights, sems) = refs[:-3], refs[-3:]
    width = grads[0].shape[1]
    rows = grads[0].shape[0] // (2 * GROUP)
    depth = GROUP * width
    per_out = outs[0].shape[0]
    here, start, in_middle = pos[0], pos[1], pos[2]

    def transfer(finish):
        for n, (source, (where, first, size, column)) in enumerate(zip(sources, parts)):

            def move():
                for c in range(2):
                    target = weights.at[c, pl.ds(column, size)]
                    sem = sems.at[n, c]
                    copy = pltpu.make_async_copy(source.at[c, pl.ds(first, size)], target, sem)
                    copy.wait() if finish else copy.start()

            if where is None:
                move()
            else:
                pl.when(in_middle == where)(move)

    transfer(False)
    transfer(True)
    for c in range(2):
        for a in range(GROUP):
            column = pl.multiple_of((here ^ a) * width, width)
            term = lax.dot_general(
                grads[a][c * GROUP * rows : (c + 1) * GROUP * rows],
                weights[c, :, pl.ds(column, width)],
                NT,
                preferred_element_type=jnp.float32,
            )
            total[...] = term if c + a == 0 else total[...] + term
    for n, out in enumerate(outs):
        for j in range(per_out):
            p = lax.rem(pos[3 + n * per_out + j] + (GROUP - 1) - start, GROUP)
            place = pl.ds(pl.multiple_of(p * rows, rows), rows)
            out[j] = total[place].astype(out.dtype)


def project(pos, rows_at, n_out, grads, parts):
    rows = grads[0].shape[0] // (2 * GROUP)
    depth = GROUP * grads[0].shape[1]
    columns = max(column + size for _, (_, _, size, column) in parts)
    half = jnp.bfloat16
    whole = pl.BlockSpec(memory_space=pltpu.VMEM)
    anywhere = pl.BlockSpec(memory_space=pl.ANY)
    count = len(rows_at)
    pos = jnp.stack(list(pos) + list(rows_at)).astype(jnp.int32)
    return pl.pallas_call(
        functools.partial(project_kernel, [part for _, part in parts]),
        out_shape=[jax.ShapeDtypeStruct((count // n_out, rows, columns), half)] * n_out,
        in_specs=[pl.BlockSpec(memory_space=pltpu.SMEM)]
        + [whole] * GROUP
        + [anywhere] * len(parts),
        out_specs=[whole] * n_out,
        scratch_shapes=[
            pltpu.VMEM((GROUP * rows, columns), jnp.float32),
            pltpu.VMEM((2, columns, depth), half),
            pltpu.SemaphoreType.DMA((len(parts), 2)),
        ],
        compiler_params=pltpu.CompilerParams(vmem_limit_bytes=20 * 2**20),
        cost_estimate=pl.CostEstimate(
            flops=4 * count * rows * columns * depth,
            bytes_accessed=6 * 2**20,
            transcendentals=0,
        ),
        name="project",
    )(pos, *grads, *[weight for weight, _ in parts])


def merge_kernel(flip, *refs):
    kept_own, given_own = refs[:2]
    n_parts = (len(refs) - 2 - 4) // 2
    kept, given, outs = refs[2 : 2 + n_parts], refs[2 + n_parts : 2 + 2 * n_parts], refs[-4:]
    for order in range(2):

        @pl.when(flip[0] == order)
        def _():
            for n, out in enumerate(outs):
                if (n % 2) ^ order == 0:
                    terms = [(kept_own, given_own)]
                else:
                    terms = list(zip(kept, given))
                column = 0
                for left, right in terms:
                    size = left.shape[2]
                    total = left[n // 2].astype(jnp.float32) + right[n // 2].astype(jnp.float32)
                    out[:, column : column + size] = total.astype(out.dtype)
                    column += size


def merge(flip, kept_own, given_own, kept, given):
    whole = pl.BlockSpec(memory_space=pltpu.VMEM)
    return pl.pallas_call(
        merge_kernel,
        out_shape=[jax.ShapeDtypeStruct(kept_own.shape[1:], kept_own.dtype)] * 4,
        in_specs=[pl.BlockSpec(memory_space=pltpu.SMEM)] + [whole] * (2 + 2 * len(kept)),
        out_specs=[whole] * 4,
        name="merge",
    )(flip, kept_own, given_own, *kept, *given)


def collect_kernel(pos, *refs):
    parts, out = refs[:-1], refs[-1]
    wide = out.shape[1] // 2
    for a in range(2):
        total = parts[2 * a][...].astype(jnp.float32) + parts[2 * a + 1][...].astype(jnp.float32)
        out[:, pl.ds(pl.multiple_of((pos[0] ^ a) * wide, wide), wide)] = total.astype(out.dtype)


def collect(pos, parts):
    rows, wide = parts[0].shape
    whole = pl.BlockSpec(memory_space=pltpu.VMEM)
    return pl.pallas_call(
        collect_kernel,
        out_shape=jax.ShapeDtypeStruct((rows, 2 * wide), parts[0].dtype),
        in_specs=[pl.BlockSpec(memory_space=pltpu.SMEM)] + [whole] * 4,
        out_specs=whole,
        name="collect",
    )(pos, *parts)


def place_kernel(pos, *refs):
    out = refs[-1]
    for a, part in enumerate(refs[:-1]):
        width = part.shape[1]
        start = pl.multiple_of((pos[0] ^ a) * width, width)
        out[:, pl.ds(start, width)] = part[...]


def place_columns(pos, parts):
    rows, width = parts[0].shape
    whole = pl.BlockSpec(memory_space=pltpu.VMEM)
    return pl.pallas_call(
        place_kernel,
        out_shape=jax.ShapeDtypeStruct((rows, GROUP * width), parts[0].dtype),
        in_specs=[pl.BlockSpec(memory_space=pltpu.SMEM)] + [whole] * len(parts),
        out_specs=whole,
        name="place_columns",
    )(pos, *parts)


def other_core(block):
    return send(block, lambda t, s: (t, s ^ 1))


def deliver(parts):
    arrived = []
    for n, part in enumerate(parts):
        a1, a2 = n // 2, n % 2

        def route(t, s):
            g, z, x = t // GROUP, (t // 2) % 2, t % 2
            y, core = s // 2, s % 2
            return (g * GROUP + 2 * core + (x ^ a1), 2 * (y ^ a2) + (z ^ y ^ a2 ^ g))

        arrived.append(send(part, route))
    return arrived


def deliver_any(parts, group):
    groups = len(parts)
    secs = lax.axis_size("sec")
    rows, wide = parts[0].shape[1:]
    stacked = jnp.roll(jnp.stack(parts[::-1]), group + 1, axis=0)
    shape = (secs, groups // secs, GROUP, rows, wide)
    mine = lax.psum_scatter(stacked.reshape(shape), "sec", scatter_dimension=0, tiled=False)
    mine = jnp.moveaxis(mine, 1, 0)
    n_tgt = lax.axis_size("tgt")
    lists = [list(range(g, g + GROUP)) for g in range(0, n_tgt, GROUP)]
    mine = lax.all_to_all(mine, "tgt", 0, 0, axis_index_groups=lists)
    return jnp.transpose(mine, (2, 1, 0, 3)).reshape(rows, -1)


def after(block, *earlier):
    return lax.optimization_barrier((block, *earlier))[0]


def per_device(queries, key_values, grad_out, block_ids, block_count, kv_weight):
    rows_here, width_here = queries.shape
    blocks_here = rows_here // BLOCK
    width = width_here // GROUP
    n_tgt = lax.axis_size("tgt")
    groups = n_tgt // GROUP
    paired = groups == 2
    n_halo = 1 if paired else 2
    t, s = lax.axis_index("tgt"), lax.axis_index("sec")
    group, here = t // GROUP, t % GROUP
    start = jnp.where(group == 0, GROUP - 1, 0) if paired else 0
    pos = jnp.stack([here, start]).astype(jnp.int32)

    def other_group(block):
        return send(block, lambda t, s: (t ^ GROUP, s))

    def middle(block):
        return send(block, lambda t, s: (t ^ 6, s) if t // 2 in (1, 2) else None)

    def ends(block):
        return send(block, lambda t, s: (t ^ 6, s) if t // 2 in (0, 3) else None)

    def shifted(block, k):
        return send(block, lambda t, s: (t + GROUP * k, s))

    wide = kv_weight.shape[1]
    unit = wide // 16
    middle_cuts, end_cuts = (0, 7, 16), (0, 12, 16)

    def rows_of(cuts, n):
        return kv_weight[:, cuts[n] * unit : cuts[n + 1] * unit]

    total = (GROUP + n_halo) * blocks_here
    packs = pack(total, block_ids, block_count, queries, grad_out, key_values)
    if paired:
        middles = [middle(after(rows_of(middle_cuts, 0), packs[0]))]
    packs = [packs[0]] + [swap(packs[a], a) for a in range(1, GROUP)]
    pairs = [p[2 * rows_here : 4 * rows_here] for p in packs]

    def member(m):
        chosen = pairs[0]
        for a in range(1, GROUP):
            chosen = jnp.where(here ^ a == m, pairs[a], chosen)
        return chosen

    if paired:
        halos = [other_group(after(member(start), middles[0]))]
    else:
        halos = [shifted(member(0), -1), shifted(member(GROUP - 1), 1)]

    meta = jnp.stack([p[4 * rows_here : 4 * rows_here + blocks_here, : SLOTS + 1] for p in packs])
    meta = meta.astype(jnp.int32)
    own = GROUP * blocks_here
    n_inner = own - n_halo * blocks_here
    state, _ = attend((0, n_inner // 2), n_halo, meta, pos, packs)
    state, backs = attend((n_inner, own), n_halo, meta, pos, packs, halos, state)
    if paired:
        returned = other_group(backs[0])
    else:
        returned = jnp.concatenate([shifted(backs[1], -1), shifted(backs[0], 1)], axis=1)
    _, results = attend((n_inner // 2, n_inner), n_halo, meta, pos, packs, (), state, True)
    dq, (inner, edge) = results[:GROUP], results[GROUP:]
    edge = (edge + returned.astype(jnp.float32)).astype(jnp.bfloat16)
    grads = jnp.concatenate([inner, edge], axis=1).reshape(-1, width)
    dq = [block.reshape(rows_here, width) for block in dq]
    if paired:
        middles.append(middle(after(rows_of(middle_cuts, 1), returned)))
    near, beside = swap(grads, 1), swap(grads, 2)
    if paired:
        far = [ends(after(rows_of(end_cuts, 0), beside, middles[1]))]
        beside = after(beside, near, middles[1])
    grads = [grads, near, beside, swap(beside, 1)]
    dq = [dq[0]] + [swap(after(dq[a], grads[3]), a) for a in range(1, GROUP)]

    if paired:
        in_middle = ((t // 2 == 1) | (t // 2 == 2)).astype(jnp.int32)
        core, y, x = s % 2, s // 2, t % 2
        pos = [here, start, in_middle]
        order = [2 * z + (x ^ a) for z in (core ^ 1, core) for a in range(2)]
        give_own, keep_own = project(pos, order, 2, grads, [(kv_weight, (None, 0, wide, 0))])
        given_own = other_core(give_own)
        far.append(ends(after(rows_of(end_cuts, 1), grads[3])))
        kept, given = [], []
        for lo, hi in zip(end_cuts, end_cuts[1:]):
            parts = []
            for where, weights, cuts in ((1, middles, middle_cuts), (0, far, end_cuts)):
                for weight, first, last in zip(weights, cuts, cuts[1:]):
                    begin, end = max(first, lo), min(last, hi)
                    if begin < end:
                        span = ((begin - first) * unit, (end - begin) * unit, (begin - lo) * unit)
                        parts.append((weight, (where,) + span))
            give_other, keep_other = project(pos, order, 2, grads, parts)
            kept.append(keep_other)
            given.append(other_core(give_other))
        kept[-1] = after(kept[-1], *dq[1:])
        flip = (y ^ group).astype(jnp.int32).reshape(1)
        arrived = deliver(merge(flip, keep_own, given_own, kept, given))
        grad_memory = collect(x.astype(jnp.int32).reshape(1), arrived)
    else:
        weights = [kv_weight] + [
            send(kv_weight, lambda t, s, k=k: ((t + GROUP * k) % n_tgt, s))
            for k in range(1, groups)
        ]
        pos, rows_at = [here, start, 0], list(range(GROUP))
        parts = [project(pos, rows_at, 1, grads, [(w, (None, 0, wide, 0))])[0] for w in weights]
        grad_memory = deliver_any(parts, group)

    here = here.astype(jnp.int32).reshape(1)
    return place_columns(here, dq), grad_memory


def solution(mesh):
    return jax.shard_map(
        per_device,
        mesh=mesh,
        in_specs=(
            P("tgt", "sec"),
            P(None, "tgt", "sec"),
            P("tgt", "sec"),
            P("tgt", None),
            P("tgt"),
            P(None, "tgt", "sec"),
        ),
        out_specs=(P("tgt", "sec"), P("tgt", "sec")),
        check_vma=False,
    )
```

```python
import functools
import math

import jax
import jax.numpy as jnp
from jax import lax
from jax.experimental import pallas as pl
from jax.experimental.pallas import tpu as pltpu
from jax.sharding import PartitionSpec as P

HEAD_DIM = 64
BLOCK = 128
SLOTS = 4
GROUP = 4
AXES = ("tgt", "sec")
SCALE = 0.125
NT = (((1,), (1,)), ((), ()))
TN = (((0,), (0,)), ((), ()))


def send(block, route):
    rows, secs = lax.axis_size("tgt"), lax.axis_size("sec")
    pairs = []
    for t in range(rows):
        for s in range(secs):
            target = route(t, s)
            if target is not None and 0 <= target[0] < rows:
                pairs.append((t * secs + s, target[0] * secs + target[1]))
    return lax.ppermute(block, AXES, pairs)


def swap(block, a):
    return send(block, lambda t, s: (t ^ a, s))


def pack_kernel(total, block_ids, block_count, queries, grad_out, key_values, *outs):
    width = outs[0].shape[1]
    size = queries.shape[0]
    position = lax.axis_index("tgt")
    here, group = lax.rem(position, GROUP), lax.div(position, GROUP)
    blocks_here, slots = block_ids.shape
    shape = (outs[0].shape[0] - 4 * size, width)
    row = lax.broadcasted_iota(jnp.int32, shape, 0)
    column = lax.broadcasted_iota(jnp.int32, shape, 1)
    lists = jnp.zeros(shape, jnp.int32)
    for r in range(blocks_here):
        for n in range(slots):
            slot = lax.rem(block_ids[r, n] - group * GROUP * blocks_here + total, total)
            lists = jnp.where((row == r) & (column == n), slot, lists)
        lists = jnp.where((row == r) & (column == slots), block_count[r], lists)
    lists = lists.astype(jnp.float32).astype(outs[0].dtype)
    for a, out in enumerate(outs):
        columns = pl.ds(pl.multiple_of((here ^ a) * width, width), width)
        out[0:size] = queries[:, columns]
        out[size : 2 * size] = grad_out[:, columns]
        out[2 * size : 3 * size] = key_values[0, :, columns]
        out[3 * size : 4 * size] = key_values[1, :, columns]
        out[4 * size :] = lists


def pack(total, block_ids, block_count, queries, grad_out, key_values):
    width = queries.shape[1] // GROUP
    shape = jax.ShapeDtypeStruct((4 * queries.shape[0] + 16, width), queries.dtype)
    whole = pl.BlockSpec(memory_space=pltpu.VMEM)
    scalars = pl.BlockSpec(memory_space=pltpu.SMEM)
    return pl.pallas_call(
        functools.partial(pack_kernel, total),
        out_shape=[shape] * GROUP,
        in_specs=[scalars] * 2 + [whole] * 3,
        out_specs=[whole] * GROUP,
        name="pack",
    )(block_ids, block_count, queries, grad_out, key_values)


def attend_kernel(span, n_halo, with_halos, with_state, last, meta, pos, *refs):
    packs, refs = refs[:GROUP], refs[GROUP:]
    n_read = n_halo if with_halos else 0
    halos, refs = refs[:n_read], refs[n_read:]
    state, refs = refs[: 2 * with_state], refs[2 * with_state :]
    outs, (keys, values, rows, ups, kg, vg, qm, om) = refs[:-8], refs[-8:]
    acc, dq_all = outs[:2]
    own, width = dq_all.shape[0], dq_all.shape[2]
    per_dev = own // GROUP
    total = own + n_halo * per_dev
    size = per_dev * BLOCK
    heads = width // HEAD_DIM
    here, start = pos[0], pos[1]
    block = (per_dev, BLOCK, width)
    for a in range(GROUP):
        place = pl.ds((here ^ a) * per_dev, per_dev)
        for n, held in enumerate((rows, ups, keys, values)):
            held[place] = packs[a][n * size : (n + 1) * size].reshape(block)
    for n, halo in enumerate(halos):
        part = slice(own + n * per_dev, own + (n + 1) * per_dev)
        keys[part] = halo[:size].reshape(block)
        values[part] = halo[size:].reshape(block)
    if not with_state:
        acc[...] = jnp.zeros_like(acc)
        dq_all[...] = jnp.zeros_like(dq_all)
    lane_head = lax.broadcasted_iota(jnp.int32, (BLOCK, width), 1) // HEAD_DIM
    key_row = lax.broadcasted_iota(jnp.int32, (SLOTS * BLOCK, heads * BLOCK), 0)

    def step(turn, carry):
        member = lax.rem(start + 1 + turn // per_dev, GROUP)
        a = here ^ member
        r = lax.rem(turn, per_dev)
        i = member * per_dev + r
        count = meta[a, r, SLOTS]
        ids = [jnp.clip(meta[a, r, s], 0, total - 1) for s in range(SLOTS)]
        for s in range(SLOTS):
            kg[s * BLOCK : (s + 1) * BLOCK] = keys[ids[s]]
            vg[s * BLOCK : (s + 1) * BLOCK] = values[ids[s]]
        q, o = rows[i], ups[i]
        for h in range(heads):
            qm[h * BLOCK : (h + 1) * BLOCK] = jnp.where(lane_head == h, q, 0)
            om[h * BLOCK : (h + 1) * BLOCK] = jnp.where(lane_head == h, o, 0)
        scores = lax.dot_general(kg[...], qm[...], NT, preferred_element_type=jnp.float32)
        scores = jnp.where(key_row < count * BLOCK, scores, -jnp.inf)
        top = jnp.max(scores, axis=0, keepdims=True)
        expo = jnp.exp2((scores - top) * (SCALE * math.log2(math.e)))
        probs = expo * (1.0 / jnp.sum(expo, axis=0, keepdims=True))
        probs_half = probs.astype(jnp.bfloat16)
        grad_probs = lax.dot_general(vg[...], om[...], NT, preferred_element_type=jnp.float32)
        delta = jnp.sum(probs_half.astype(jnp.float32) * grad_probs, axis=0, keepdims=True)
        grad_half = (probs * (grad_probs - delta)).astype(jnp.bfloat16)
        grad_value = jnp.dot(probs_half, om[...], preferred_element_type=jnp.float32)
        grad_key = SCALE * jnp.dot(grad_half, qm[...], preferred_element_type=jnp.float32)
        for s in range(SLOTS):
            part = slice(s * BLOCK, (s + 1) * BLOCK)
            acc[0, ids[s]] += grad_key[part]
            acc[1, ids[s]] += grad_value[part]
        flipped = lax.dot_general(kg[...], grad_half, TN, preferred_element_type=jnp.float32)
        flipped = jnp.concatenate(
            [
                flipped[h * HEAD_DIM : (h + 1) * HEAD_DIM, h * BLOCK : (h + 1) * BLOCK]
                for h in range(heads)
            ],
            axis=0,
        )
        dq_all[i] = (SCALE * flipped.T).astype(jnp.bfloat16)
        return carry

    lax.fori_loop(span[0], span[1], step, 0)
    half = jnp.bfloat16
    if last:
        dq_outs, (inner, edge) = outs[2 : 2 + GROUP], outs[2 + GROUP :]
        for a in range(GROUP):
            dq_outs[a][...] = dq_all[pl.ds((here ^ a) * per_dev, per_dev)]
        for p in range(GROUP):
            member = lax.rem(start + 1 + p, GROUP)
            taken = acc[:, pl.ds(member * per_dev, per_dev)]
            if p < GROUP - n_halo:
                inner[:, p * per_dev : (p + 1) * per_dev] = taken.astype(half)
            else:
                p -= GROUP - n_halo
                edge[:, p * per_dev : (p + 1) * per_dev] = taken
    elif with_halos:
        for n, back in enumerate(outs[2:]):
            part = slice(own + n * per_dev, own + (n + 1) * per_dev)
            back[...] = acc[:, part].astype(half)


def attend(span, n_halo, meta, pos, packs, halos=(), state=(), last=False):
    per_dev, width = meta.shape[1], packs[0].shape[1]
    own = GROUP * per_dev
    total = own + n_halo * per_dev
    heads = width // HEAD_DIM
    half = jnp.bfloat16
    block = (BLOCK, width)
    shapes = [
        jax.ShapeDtypeStruct((2, total) + block, jnp.float32),
        jax.ShapeDtypeStruct((own,) + block, half),
    ]
    if last:
        shapes += [jax.ShapeDtypeStruct((per_dev,) + block, half)] * GROUP
        shapes.append(jax.ShapeDtypeStruct((2, own - n_halo * per_dev) + block, half))
        shapes.append(jax.ShapeDtypeStruct((2, n_halo * per_dev) + block, jnp.float32))
    elif halos:
        shapes += [jax.ShapeDtypeStruct((2, per_dev) + block, half)] * n_halo
    scratch = (
        [pltpu.VMEM((total,) + block, half)] * 2
        + [pltpu.VMEM((own,) + block, half)] * 2
        + [pltpu.VMEM((SLOTS * BLOCK, width), half)] * 2
        + [pltpu.VMEM((heads * BLOCK, width), half)] * 2
    )
    whole = pl.BlockSpec(memory_space=pltpu.VMEM)
    scalars = pl.BlockSpec(memory_space=pltpu.SMEM)
    turns = span[1] - span[0]
    results = pl.pallas_call(
        functools.partial(attend_kernel, span, n_halo, bool(halos), bool(state), last),
        out_shape=shapes,
        in_specs=[scalars] * 2 + [whole] * (GROUP + len(halos) + len(state)),
        out_specs=[whole] * len(shapes),
        scratch_shapes=scratch,
        input_output_aliases={2 + GROUP + len(halos) + n: n for n in range(len(state))},
        compiler_params=pltpu.CompilerParams(vmem_limit_bytes=20 * 2**20),
        cost_estimate=pl.CostEstimate(
            flops=turns * 10 * SLOTS * BLOCK * heads * BLOCK * width,
            bytes_accessed=4 * 2**20,
            transcendentals=turns * SLOTS * heads * BLOCK * BLOCK,
        ),
        name="attend",
    )(meta, pos, *packs, *halos, *state)
    return results[:2], results[2:]


def project_kernel(parts, pos, *refs):
    grads, sources, refs = refs[:GROUP], refs[GROUP : GROUP + len(parts)], refs[GROUP + len(parts) :]
    outs, (total, weights, sems) = refs[:-3], refs[-3:]
    width = grads[0].shape[1]
    rows = grads[0].shape[0] // (2 * GROUP)
    depth = GROUP * width
    per_out = outs[0].shape[0]
    here, start, in_middle = pos[0], pos[1], pos[2]

    def transfer(finish):
        for n, (source, (where, first, size, column)) in enumerate(zip(sources, parts)):

            def move():
                for c in range(2):
                    target = weights.at[c, pl.ds(column, size)]
                    sem = sems.at[n, c]
                    copy = pltpu.make_async_copy(source.at[c, pl.ds(first, size)], target, sem)
                    copy.wait() if finish else copy.start()

            if where is None:
                move()
            else:
                pl.when(in_middle == where)(move)

    transfer(False)
    transfer(True)
    for c in range(2):
        for a in range(GROUP):
            column = pl.multiple_of((here ^ a) * width, width)
            term = lax.dot_general(
                grads[a][c * GROUP * rows : (c + 1) * GROUP * rows],
                weights[c, :, pl.ds(column, width)],
                NT,
                preferred_element_type=jnp.float32,
            )
            total[...] = term if c + a == 0 else total[...] + term
    for n, out in enumerate(outs):
        for j in range(per_out):
            p = lax.rem(pos[3 + n * per_out + j] + (GROUP - 1) - start, GROUP)
            place = pl.ds(pl.multiple_of(p * rows, rows), rows)
            out[j] = total[place].astype(out.dtype)


def project(pos, rows_at, n_out, grads, parts):
    rows = grads[0].shape[0] // (2 * GROUP)
    depth = GROUP * grads[0].shape[1]
    columns = max(column + size for _, (_, _, size, column) in parts)
    half = jnp.bfloat16
    whole = pl.BlockSpec(memory_space=pltpu.VMEM)
    anywhere = pl.BlockSpec(memory_space=pl.ANY)
    count = len(rows_at)
    pos = jnp.stack(list(pos) + list(rows_at)).astype(jnp.int32)
    return pl.pallas_call(
        functools.partial(project_kernel, [part for _, part in parts]),
        out_shape=[jax.ShapeDtypeStruct((count // n_out, rows, columns), half)] * n_out,
        in_specs=[pl.BlockSpec(memory_space=pltpu.SMEM)]
        + [whole] * GROUP
        + [anywhere] * len(parts),
        out_specs=[whole] * n_out,
        scratch_shapes=[
            pltpu.VMEM((GROUP * rows, columns), jnp.float32),
            pltpu.VMEM((2, columns, depth), half),
            pltpu.SemaphoreType.DMA((len(parts), 2)),
        ],
        compiler_params=pltpu.CompilerParams(vmem_limit_bytes=20 * 2**20),
        cost_estimate=pl.CostEstimate(
            flops=4 * count * rows * columns * depth,
            bytes_accessed=6 * 2**20,
            transcendentals=0,
        ),
        name="project",
    )(pos, *grads, *[weight for weight, _ in parts])


def merge_kernel(flip, *refs):
    kept_own, given_own = refs[:2]
    n_parts = (len(refs) - 2 - 4) // 2
    kept, given, outs = refs[2 : 2 + n_parts], refs[2 + n_parts : 2 + 2 * n_parts], refs[-4:]
    for order in range(2):

        @pl.when(flip[0] == order)
        def _():
            for n, out in enumerate(outs):
                if (n % 2) ^ order == 0:
                    terms = [(kept_own, given_own)]
                else:
                    terms = list(zip(kept, given))
                column = 0
                for left, right in terms:
                    size = left.shape[2]
                    total = left[n // 2].astype(jnp.float32) + right[n // 2].astype(jnp.float32)
                    out[:, column : column + size] = total.astype(out.dtype)
                    column += size


def merge(flip, kept_own, given_own, kept, given):
    whole = pl.BlockSpec(memory_space=pltpu.VMEM)
    return pl.pallas_call(
        merge_kernel,
        out_shape=[jax.ShapeDtypeStruct(kept_own.shape[1:], kept_own.dtype)] * 4,
        in_specs=[pl.BlockSpec(memory_space=pltpu.SMEM)] + [whole] * (2 + 2 * len(kept)),
        out_specs=[whole] * 4,
        name="merge",
    )(flip, kept_own, given_own, *kept, *given)


def collect_kernel(pos, *refs):
    parts, out = refs[:-1], refs[-1]
    wide = out.shape[1] // 2
    for a in range(2):
        total = parts[2 * a][...].astype(jnp.float32) + parts[2 * a + 1][...].astype(jnp.float32)
        out[:, pl.ds(pl.multiple_of((pos[0] ^ a) * wide, wide), wide)] = total.astype(out.dtype)


def collect(pos, parts):
    rows, wide = parts[0].shape
    whole = pl.BlockSpec(memory_space=pltpu.VMEM)
    return pl.pallas_call(
        collect_kernel,
        out_shape=jax.ShapeDtypeStruct((rows, 2 * wide), parts[0].dtype),
        in_specs=[pl.BlockSpec(memory_space=pltpu.SMEM)] + [whole] * 4,
        out_specs=whole,
        name="collect",
    )(pos, *parts)


def place_kernel(pos, *refs):
    out = refs[-1]
    for a, part in enumerate(refs[:-1]):
        width = part.shape[1]
        start = pl.multiple_of((pos[0] ^ a) * width, width)
        out[:, pl.ds(start, width)] = part[...]


def place_columns(pos, parts):
    rows, width = parts[0].shape
    whole = pl.BlockSpec(memory_space=pltpu.VMEM)
    return pl.pallas_call(
        place_kernel,
        out_shape=jax.ShapeDtypeStruct((rows, GROUP * width), parts[0].dtype),
        in_specs=[pl.BlockSpec(memory_space=pltpu.SMEM)] + [whole] * len(parts),
        out_specs=whole,
        name="place_columns",
    )(pos, *parts)


def other_core(block):
    return send(block, lambda t, s: (t, s ^ 1))


def deliver(parts):
    arrived = []
    for n, part in enumerate(parts):
        a1, a2 = n // 2, n % 2

        def route(t, s):
            g, z, x = t // GROUP, (t // 2) % 2, t % 2
            y, core = s // 2, s % 2
            return (g * GROUP + 2 * core + (x ^ a1), 2 * (y ^ a2) + (z ^ y ^ a2 ^ g))

        arrived.append(send(part, route))
    return arrived


def deliver_any(parts, group):
    groups = len(parts)
    secs = lax.axis_size("sec")
    rows, wide = parts[0].shape[1:]
    stacked = jnp.roll(jnp.stack(parts[::-1]), group + 1, axis=0)
    shape = (secs, groups // secs, GROUP, rows, wide)
    mine = lax.psum_scatter(stacked.reshape(shape), "sec", scatter_dimension=0, tiled=False)
    mine = jnp.moveaxis(mine, 1, 0)
    n_tgt = lax.axis_size("tgt")
    lists = [list(range(g, g + GROUP)) for g in range(0, n_tgt, GROUP)]
    mine = lax.all_to_all(mine, "tgt", 0, 0, axis_index_groups=lists)
    return jnp.transpose(mine, (2, 1, 0, 3)).reshape(rows, -1)


def after(block, *earlier):
    return lax.optimization_barrier((block, *earlier))[0]


def per_device(queries, key_values, grad_out, block_ids, block_count, kv_weight):
    rows_here, width_here = queries.shape
    blocks_here = rows_here // BLOCK
    width = width_here // GROUP
    n_tgt = lax.axis_size("tgt")
    groups = n_tgt // GROUP
    paired = groups == 2
    n_halo = 1 if paired else 2
    t, s = lax.axis_index("tgt"), lax.axis_index("sec")
    group, here = t // GROUP, t % GROUP
    start = jnp.where(group == 0, GROUP - 1, 0) if paired else 0
    pos = jnp.stack([here, start]).astype(jnp.int32)

    def other_group(block):
        return send(block, lambda t, s: (t ^ GROUP, s))

    def middle(block):
        return send(block, lambda t, s: (t ^ 6, s) if t // 2 in (1, 2) else None)

    def ends(block):
        return send(block, lambda t, s: (t ^ 6, s) if t // 2 in (0, 3) else None)

    def shifted(block, k):
        return send(block, lambda t, s: (t + GROUP * k, s))

    wide = kv_weight.shape[1]
    unit = wide // 16
    middle_cuts, end_cuts = (0, 7, 16), (0, 12, 16)

    def rows_of(cuts, n):
        return kv_weight[:, cuts[n] * unit : cuts[n + 1] * unit]

    total = (GROUP + n_halo) * blocks_here
    packs = pack(total, block_ids, block_count, queries, grad_out, key_values)
    if paired:
        middles = [middle(after(rows_of(middle_cuts, 0), packs[0]))]
    packs = [packs[0]] + [swap(packs[a], a) for a in range(1, GROUP)]
    pairs = [p[2 * rows_here : 4 * rows_here] for p in packs]

    def member(m):
        chosen = pairs[0]
        for a in range(1, GROUP):
            chosen = jnp.where(here ^ a == m, pairs[a], chosen)
        return chosen

    if paired:
        halos = [other_group(after(member(start), middles[0]))]
    else:
        halos = [shifted(member(0), -1), shifted(member(GROUP - 1), 1)]

    meta = jnp.stack([p[4 * rows_here : 4 * rows_here + blocks_here, : SLOTS + 1] for p in packs])
    meta = meta.astype(jnp.int32)
    own = GROUP * blocks_here
    n_inner = own - n_halo * blocks_here
    state, _ = attend((0, n_inner // 2), n_halo, meta, pos, packs)
    state, backs = attend((n_inner, own), n_halo, meta, pos, packs, halos, state)
    if paired:
        returned = other_group(backs[0])
    else:
        returned = jnp.concatenate([shifted(backs[1], -1), shifted(backs[0], 1)], axis=1)
    _, results = attend((n_inner // 2, n_inner), n_halo, meta, pos, packs, (), state, True)
    dq, (inner, edge) = results[:GROUP], results[GROUP:]
    edge = (edge + returned.astype(jnp.float32)).astype(jnp.bfloat16)
    grads = jnp.concatenate([inner, edge], axis=1).reshape(-1, width)
    dq = [block.reshape(rows_here, width) for block in dq]
    if paired:
        middles.append(middle(after(rows_of(middle_cuts, 1), inner)))
    near = swap(grads, 1)
    beside = jnp.concatenate([swap(inner, 2), swap(edge, 2)], axis=1).reshape(-1, width)
    if paired:
        far = [ends(after(rows_of(end_cuts, 0), beside, middles[1]))]
        beside = after(beside, near, middles[1])
    grads = [grads, near, beside, swap(beside, 1)]
    dq = [dq[0]] + [swap(after(dq[a], grads[3]), a) for a in range(1, GROUP)]

    if paired:
        in_middle = ((t // 2 == 1) | (t // 2 == 2)).astype(jnp.int32)
        core, y, x = s % 2, s // 2, t % 2
        pos = [here, start, in_middle]
        order = [2 * z + (x ^ a) for z in (core ^ 1, core) for a in range(2)]
        give_own, keep_own = project(pos, order, 2, grads, [(kv_weight, (None, 0, wide, 0))])
        given_own = other_core(give_own)
        far.append(ends(after(rows_of(end_cuts, 1), grads[3])))
        kept, given = [], []
        for lo, hi in zip(end_cuts, end_cuts[1:]):
            parts = []
            for where, weights, cuts in ((1, middles, middle_cuts), (0, far, end_cuts)):
                for weight, first, last in zip(weights, cuts, cuts[1:]):
                    begin, end = max(first, lo), min(last, hi)
                    if begin < end:
                        span = ((begin - first) * unit, (end - begin) * unit, (begin - lo) * unit)
                        parts.append((weight, (where,) + span))
            give_other, keep_other = project(pos, order, 2, grads, parts)
            kept.append(keep_other)
            given.append(other_core(give_other))
        kept[-1] = after(kept[-1], *dq[1:])
        flip = (y ^ group).astype(jnp.int32).reshape(1)
        arrived = deliver(merge(flip, keep_own, given_own, kept, given))
        grad_memory = collect(x.astype(jnp.int32).reshape(1), arrived)
    else:
        weights = [kv_weight] + [
            send(kv_weight, lambda t, s, k=k: ((t + GROUP * k) % n_tgt, s))
            for k in range(1, groups)
        ]
        pos, rows_at = [here, start, 0], list(range(GROUP))
        parts = [project(pos, rows_at, 1, grads, [(w, (None, 0, wide, 0))])[0] for w in weights]
        grad_memory = deliver_any(parts, group)

    here = here.astype(jnp.int32).reshape(1)
    return place_columns(here, dq), grad_memory


def solution(mesh):
    return jax.shard_map(
        per_device,
        mesh=mesh,
        in_specs=(
            P("tgt", "sec"),
            P(None, "tgt", "sec"),
            P("tgt", "sec"),
            P("tgt", None),
            P("tgt"),
            P(None, "tgt", "sec"),
        ),
        out_specs=(P("tgt", "sec"), P("tgt", "sec")),
        check_vma=False,
    )
```

```python
import functools
import math

import jax
import jax.numpy as jnp
from jax import lax
from jax.experimental import pallas as pl
from jax.experimental.pallas import tpu as pltpu
from jax.sharding import PartitionSpec as P

HEAD_DIM = 64
BLOCK = 128
SLOTS = 4
GROUP = 4
AXES = ("tgt", "sec")
SCALE = 0.125
NT = (((1,), (1,)), ((), ()))
TN = (((0,), (0,)), ((), ()))


def send(block, route):
    rows, secs = lax.axis_size("tgt"), lax.axis_size("sec")
    pairs = []
    for t in range(rows):
        for s in range(secs):
            target = route(t, s)
            if target is not None and 0 <= target[0] < rows:
                pairs.append((t * secs + s, target[0] * secs + target[1]))
    return lax.ppermute(block, AXES, pairs)


def swap(block, a):
    return send(block, lambda t, s: (t ^ a, s))


def pack_kernel(total, block_ids, block_count, queries, grad_out, key_values, *outs):
    width = outs[0].shape[1]
    size = queries.shape[0]
    position = lax.axis_index("tgt")
    here, group = lax.rem(position, GROUP), lax.div(position, GROUP)
    blocks_here, slots = block_ids.shape
    shape = (outs[0].shape[0] - 4 * size, width)
    row = lax.broadcasted_iota(jnp.int32, shape, 0)
    column = lax.broadcasted_iota(jnp.int32, shape, 1)
    lists = jnp.zeros(shape, jnp.int32)
    for r in range(blocks_here):
        for n in range(slots):
            slot = lax.rem(block_ids[r, n] - group * GROUP * blocks_here + total, total)
            lists = jnp.where((row == r) & (column == n), slot, lists)
        lists = jnp.where((row == r) & (column == slots), block_count[r], lists)
    lists = lists.astype(jnp.float32).astype(outs[0].dtype)
    for a, out in enumerate(outs):
        columns = pl.ds(pl.multiple_of((here ^ a) * width, width), width)
        out[0:size] = queries[:, columns]
        out[size : 2 * size] = grad_out[:, columns]
        out[2 * size : 3 * size] = key_values[0, :, columns]
        out[3 * size : 4 * size] = key_values[1, :, columns]
        out[4 * size :] = lists


def pack(total, block_ids, block_count, queries, grad_out, key_values):
    width = queries.shape[1] // GROUP
    shape = jax.ShapeDtypeStruct((4 * queries.shape[0] + 16, width), queries.dtype)
    whole = pl.BlockSpec(memory_space=pltpu.VMEM)
    scalars = pl.BlockSpec(memory_space=pltpu.SMEM)
    return pl.pallas_call(
        functools.partial(pack_kernel, total),
        out_shape=[shape] * GROUP,
        in_specs=[scalars] * 2 + [whole] * 3,
        out_specs=[whole] * GROUP,
        name="pack",
    )(block_ids, block_count, queries, grad_out, key_values)


def attend_kernel(span, n_halo, with_halos, with_state, last, meta, pos, *refs):
    packs, refs = refs[:GROUP], refs[GROUP:]
    n_read = n_halo if with_halos else 0
    halos, refs = refs[:n_read], refs[n_read:]
    state, refs = refs[: 2 * with_state], refs[2 * with_state :]
    outs, (keys, values, rows, ups, kg, vg, qm, om) = refs[:-8], refs[-8:]
    acc, dq_all = outs[:2]
    own, width = dq_all.shape[0], dq_all.shape[2]
    per_dev = own // GROUP
    total = own + n_halo * per_dev
    size = per_dev * BLOCK
    heads = width // HEAD_DIM
    here, start = pos[0], pos[1]
    block = (per_dev, BLOCK, width)
    for a in range(GROUP):
        place = pl.ds((here ^ a) * per_dev, per_dev)
        for n, held in enumerate((rows, ups, keys, values)):
            held[place] = packs[a][n * size : (n + 1) * size].reshape(block)
    for n, halo in enumerate(halos):
        part = slice(own + n * per_dev, own + (n + 1) * per_dev)
        keys[part] = halo[:size].reshape(block)
        values[part] = halo[size:].reshape(block)
    if with_state:
        acc[...] = state[0][...]
        dq_all[...] = state[1][...]
    else:
        acc[...] = jnp.zeros_like(acc)
        dq_all[...] = jnp.zeros_like(dq_all)
    lane_head = lax.broadcasted_iota(jnp.int32, (BLOCK, width), 1) // HEAD_DIM
    key_row = lax.broadcasted_iota(jnp.int32, (SLOTS * BLOCK, heads * BLOCK), 0)

    def step(turn, carry):
        member = lax.rem(start + 1 + turn // per_dev, GROUP)
        a = here ^ member
        r = lax.rem(turn, per_dev)
        i = member * per_dev + r
        count = meta[a, r, SLOTS]
        ids = [jnp.clip(meta[a, r, s], 0, total - 1) for s in range(SLOTS)]
        for s in range(SLOTS):
            kg[s * BLOCK : (s + 1) * BLOCK] = keys[ids[s]]
            vg[s * BLOCK : (s + 1) * BLOCK] = values[ids[s]]
        q, o = rows[i], ups[i]
        for h in range(heads):
            qm[h * BLOCK : (h + 1) * BLOCK] = jnp.where(lane_head == h, q, 0)
            om[h * BLOCK : (h + 1) * BLOCK] = jnp.where(lane_head == h, o, 0)
        scores = lax.dot_general(kg[...], qm[...], NT, preferred_element_type=jnp.float32)
        scores = jnp.where(key_row < count * BLOCK, scores, -jnp.inf)
        top = jnp.max(scores, axis=0, keepdims=True)
        expo = jnp.exp2((scores - top) * (SCALE * math.log2(math.e)))
        probs = expo * (1.0 / jnp.sum(expo, axis=0, keepdims=True))
        probs_half = probs.astype(jnp.bfloat16)
        grad_probs = lax.dot_general(vg[...], om[...], NT, preferred_element_type=jnp.float32)
        delta = jnp.sum(probs_half.astype(jnp.float32) * grad_probs, axis=0, keepdims=True)
        grad_half = (probs * (grad_probs - delta)).astype(jnp.bfloat16)
        grad_value = jnp.dot(probs_half, om[...], preferred_element_type=jnp.float32)
        grad_key = SCALE * jnp.dot(grad_half, qm[...], preferred_element_type=jnp.float32)
        for s in range(SLOTS):
            part = slice(s * BLOCK, (s + 1) * BLOCK)
            acc[0, ids[s]] += grad_key[part]
            acc[1, ids[s]] += grad_value[part]
        flipped = lax.dot_general(kg[...], grad_half, TN, preferred_element_type=jnp.float32)
        flipped = jnp.concatenate(
            [
                flipped[h * HEAD_DIM : (h + 1) * HEAD_DIM, h * BLOCK : (h + 1) * BLOCK]
                for h in range(heads)
            ],
            axis=0,
        )
        dq_all[i] = (SCALE * flipped.T).astype(jnp.bfloat16)
        return carry

    lax.fori_loop(span[0], span[1], step, 0)
    half = jnp.bfloat16
    if last:
        dq_outs, (inner, edge) = outs[2 : 2 + GROUP], outs[2 + GROUP :]
        for a in range(GROUP):
            dq_outs[a][...] = dq_all[pl.ds((here ^ a) * per_dev, per_dev)]
        for p in range(GROUP):
            member = lax.rem(start + 1 + p, GROUP)
            taken = acc[:, pl.ds(member * per_dev, per_dev)]
            if p < GROUP - n_halo:
                inner[:, p * per_dev : (p + 1) * per_dev] = taken.astype(half)
            else:
                p -= GROUP - n_halo
                edge[:, p * per_dev : (p + 1) * per_dev] = taken
    elif with_halos:
        for n, back in enumerate(outs[2:]):
            part = slice(own + n * per_dev, own + (n + 1) * per_dev)
            back[...] = acc[:, part].astype(half)


def attend(span, n_halo, meta, pos, packs, halos=(), state=(), last=False):
    per_dev, width = meta.shape[1], packs[0].shape[1]
    own = GROUP * per_dev
    total = own + n_halo * per_dev
    heads = width // HEAD_DIM
    half = jnp.bfloat16
    block = (BLOCK, width)
    shapes = [
        jax.ShapeDtypeStruct((2, total) + block, jnp.float32),
        jax.ShapeDtypeStruct((own,) + block, half),
    ]
    if last:
        shapes += [jax.ShapeDtypeStruct((per_dev,) + block, half)] * GROUP
        shapes.append(jax.ShapeDtypeStruct((2, own - n_halo * per_dev) + block, half))
        shapes.append(jax.ShapeDtypeStruct((2, n_halo * per_dev) + block, jnp.float32))
    elif halos:
        shapes += [jax.ShapeDtypeStruct((2, per_dev) + block, half)] * n_halo
    scratch = (
        [pltpu.VMEM((total,) + block, half)] * 2
        + [pltpu.VMEM((own,) + block, half)] * 2
        + [pltpu.VMEM((SLOTS * BLOCK, width), half)] * 2
        + [pltpu.VMEM((heads * BLOCK, width), half)] * 2
    )
    whole = pl.BlockSpec(memory_space=pltpu.VMEM)
    scalars = pl.BlockSpec(memory_space=pltpu.SMEM)
    turns = span[1] - span[0]
    results = pl.pallas_call(
        functools.partial(attend_kernel, span, n_halo, bool(halos), bool(state), last),
        out_shape=shapes,
        in_specs=[scalars] * 2 + [whole] * (GROUP + len(halos) + len(state)),
        out_specs=[whole] * len(shapes),
        scratch_shapes=scratch,
        compiler_params=pltpu.CompilerParams(vmem_limit_bytes=20 * 2**20),
        cost_estimate=pl.CostEstimate(
            flops=turns * 10 * SLOTS * BLOCK * heads * BLOCK * width,
            bytes_accessed=4 * 2**20,
            transcendentals=turns * SLOTS * heads * BLOCK * BLOCK,
        ),
        name="attend",
    )(meta, pos, *packs, *halos, *state)
    return results[:2], results[2:]


def project_kernel(parts, pos, *refs):
    grads, sources, refs = refs[:GROUP], refs[GROUP : GROUP + len(parts)], refs[GROUP + len(parts) :]
    outs, (total, weights, sems) = refs[:-3], refs[-3:]
    width = grads[0].shape[1]
    rows = grads[0].shape[0] // (2 * GROUP)
    depth = GROUP * width
    per_out = outs[0].shape[0]
    here, start, in_middle = pos[0], pos[1], pos[2]

    def transfer(finish):
        for n, (source, (where, first, size, column)) in enumerate(zip(sources, parts)):

            def move():
                for c in range(2):
                    target = weights.at[c, pl.ds(column, size)]
                    sem = sems.at[n, c]
                    copy = pltpu.make_async_copy(source.at[c, pl.ds(first, size)], target, sem)
                    copy.wait() if finish else copy.start()

            if where is None:
                move()
            else:
                pl.when(in_middle == where)(move)

    transfer(False)
    transfer(True)
    for c in range(2):
        for a in range(GROUP):
            column = pl.multiple_of((here ^ a) * width, width)
            term = lax.dot_general(
                grads[a][c * GROUP * rows : (c + 1) * GROUP * rows],
                weights[c, :, pl.ds(column, width)],
                NT,
                preferred_element_type=jnp.float32,
            )
            total[...] = term if c + a == 0 else total[...] + term
    for n, out in enumerate(outs):
        for j in range(per_out):
            p = lax.rem(pos[3 + n * per_out + j] + (GROUP - 1) - start, GROUP)
            place = pl.ds(pl.multiple_of(p * rows, rows), rows)
            out[j] = total[place].astype(out.dtype)


def project(pos, rows_at, n_out, grads, parts):
    rows = grads[0].shape[0] // (2 * GROUP)
    depth = GROUP * grads[0].shape[1]
    columns = max(column + size for _, (_, _, size, column) in parts)
    half = jnp.bfloat16
    whole = pl.BlockSpec(memory_space=pltpu.VMEM)
    anywhere = pl.BlockSpec(memory_space=pl.ANY)
    count = len(rows_at)
    pos = jnp.stack(list(pos) + list(rows_at)).astype(jnp.int32)
    return pl.pallas_call(
        functools.partial(project_kernel, [part for _, part in parts]),
        out_shape=[jax.ShapeDtypeStruct((count // n_out, rows, columns), half)] * n_out,
        in_specs=[pl.BlockSpec(memory_space=pltpu.SMEM)]
        + [whole] * GROUP
        + [anywhere] * len(parts),
        out_specs=[whole] * n_out,
        scratch_shapes=[
            pltpu.VMEM((GROUP * rows, columns), jnp.float32),
            pltpu.VMEM((2, columns, depth), half),
            pltpu.SemaphoreType.DMA((len(parts), 2)),
        ],
        compiler_params=pltpu.CompilerParams(vmem_limit_bytes=20 * 2**20),
        cost_estimate=pl.CostEstimate(
            flops=4 * count * rows * columns * depth,
            bytes_accessed=6 * 2**20,
            transcendentals=0,
        ),
        name="project",
    )(pos, *grads, *[weight for weight, _ in parts])


def merge_kernel(flip, *refs):
    kept_own, given_own = refs[:2]
    n_parts = (len(refs) - 2 - 4) // 2
    kept, given, outs = refs[2 : 2 + n_parts], refs[2 + n_parts : 2 + 2 * n_parts], refs[-4:]
    for order in range(2):

        @pl.when(flip[0] == order)
        def _():
            for n, out in enumerate(outs):
                if (n % 2) ^ order == 0:
                    terms = [(kept_own, given_own)]
                else:
                    terms = list(zip(kept, given))
                column = 0
                for left, right in terms:
                    size = left.shape[2]
                    total = left[n // 2].astype(jnp.float32) + right[n // 2].astype(jnp.float32)
                    out[:, column : column + size] = total.astype(out.dtype)
                    column += size


def merge(flip, kept_own, given_own, kept, given):
    whole = pl.BlockSpec(memory_space=pltpu.VMEM)
    return pl.pallas_call(
        merge_kernel,
        out_shape=[jax.ShapeDtypeStruct(kept_own.shape[1:], kept_own.dtype)] * 4,
        in_specs=[pl.BlockSpec(memory_space=pltpu.SMEM)] + [whole] * (2 + 2 * len(kept)),
        out_specs=[whole] * 4,
        name="merge",
    )(flip, kept_own, given_own, *kept, *given)


def collect_kernel(pos, *refs):
    parts, out = refs[:-1], refs[-1]
    wide = out.shape[1] // 2
    for a in range(2):
        total = parts[2 * a][...].astype(jnp.float32) + parts[2 * a + 1][...].astype(jnp.float32)
        out[:, pl.ds(pl.multiple_of((pos[0] ^ a) * wide, wide), wide)] = total.astype(out.dtype)


def collect(pos, parts):
    rows, wide = parts[0].shape
    whole = pl.BlockSpec(memory_space=pltpu.VMEM)
    return pl.pallas_call(
        collect_kernel,
        out_shape=jax.ShapeDtypeStruct((rows, 2 * wide), parts[0].dtype),
        in_specs=[pl.BlockSpec(memory_space=pltpu.SMEM)] + [whole] * 4,
        out_specs=whole,
        name="collect",
    )(pos, *parts)


def place_kernel(pos, *refs):
    out = refs[-1]
    for a, part in enumerate(refs[:-1]):
        width = part.shape[1]
        start = pl.multiple_of((pos[0] ^ a) * width, width)
        out[:, pl.ds(start, width)] = part[...]


def place_columns(pos, parts):
    rows, width = parts[0].shape
    whole = pl.BlockSpec(memory_space=pltpu.VMEM)
    return pl.pallas_call(
        place_kernel,
        out_shape=jax.ShapeDtypeStruct((rows, GROUP * width), parts[0].dtype),
        in_specs=[pl.BlockSpec(memory_space=pltpu.SMEM)] + [whole] * len(parts),
        out_specs=whole,
        name="place_columns",
    )(pos, *parts)


def other_core(block):
    return send(block, lambda t, s: (t, s ^ 1))


def deliver(parts):
    arrived = []
    for n, part in enumerate(parts):
        a1, a2 = n // 2, n % 2

        def route(t, s):
            g, z, x = t // GROUP, (t // 2) % 2, t % 2
            y, core = s // 2, s % 2
            return (g * GROUP + 2 * core + (x ^ a1), 2 * (y ^ a2) + (z ^ y ^ a2 ^ g))

        arrived.append(send(part, route))
    return arrived


def deliver_any(parts, group):
    groups = len(parts)
    secs = lax.axis_size("sec")
    rows, wide = parts[0].shape[1:]
    stacked = jnp.roll(jnp.stack(parts[::-1]), group + 1, axis=0)
    shape = (secs, groups // secs, GROUP, rows, wide)
    mine = lax.psum_scatter(stacked.reshape(shape), "sec", scatter_dimension=0, tiled=False)
    mine = jnp.moveaxis(mine, 1, 0)
    n_tgt = lax.axis_size("tgt")
    lists = [list(range(g, g + GROUP)) for g in range(0, n_tgt, GROUP)]
    mine = lax.all_to_all(mine, "tgt", 0, 0, axis_index_groups=lists)
    return jnp.transpose(mine, (2, 1, 0, 3)).reshape(rows, -1)


def after(block, *earlier):
    return lax.optimization_barrier((block, *earlier))[0]


def per_device(queries, key_values, grad_out, block_ids, block_count, kv_weight):
    rows_here, width_here = queries.shape
    blocks_here = rows_here // BLOCK
    width = width_here // GROUP
    n_tgt = lax.axis_size("tgt")
    groups = n_tgt // GROUP
    paired = groups == 2
    n_halo = 1 if paired else 2
    t, s = lax.axis_index("tgt"), lax.axis_index("sec")
    group, here = t // GROUP, t % GROUP
    start = jnp.where(group == 0, GROUP - 1, 0) if paired else 0
    pos = jnp.stack([here, start]).astype(jnp.int32)

    def other_group(block):
        return send(block, lambda t, s: (t ^ GROUP, s))

    def middle(block):
        return send(block, lambda t, s: (t ^ 6, s) if t // 2 in (1, 2) else None)

    def ends(block):
        return send(block, lambda t, s: (t ^ 6, s) if t // 2 in (0, 3) else None)

    def shifted(block, k):
        return send(block, lambda t, s: (t + GROUP * k, s))

    wide = kv_weight.shape[1]
    unit = wide // 16
    middle_cuts, end_cuts = (0, 7, 16), (0, 12, 16)

    def rows_of(cuts, n):
        return kv_weight[:, cuts[n] * unit : cuts[n + 1] * unit]

    total = (GROUP + n_halo) * blocks_here
    packs = pack(total, block_ids, block_count, queries, grad_out, key_values)
    if paired:
        middles = [middle(after(rows_of(middle_cuts, 0), packs[0]))]
    packs = [packs[0]] + [swap(packs[a], a) for a in range(1, GROUP)]
    pairs = [p[2 * rows_here : 4 * rows_here] for p in packs]

    def member(m):
        chosen = pairs[0]
        for a in range(1, GROUP):
            chosen = jnp.where(here ^ a == m, pairs[a], chosen)
        return chosen

    if paired:
        halos = [other_group(after(member(start), middles[0]))]
    else:
        halos = [shifted(member(0), -1), shifted(member(GROUP - 1), 1)]

    meta = jnp.stack([p[4 * rows_here : 4 * rows_here + blocks_here, : SLOTS + 1] for p in packs])
    meta = meta.astype(jnp.int32)
    own = GROUP * blocks_here
    n_inner = own - n_halo * blocks_here
    state, _ = attend((0, n_inner // 2), n_halo, meta, pos, packs)
    state, backs = attend((n_inner, own), n_halo, meta, pos, packs, halos, state)
    if paired:
        returned = other_group(backs[0])
    else:
        returned = jnp.concatenate([shifted(backs[1], -1), shifted(backs[0], 1)], axis=1)
    _, results = attend((n_inner // 2, n_inner), n_halo, meta, pos, packs, (), state, True)
    dq, (inner, edge) = results[:GROUP], results[GROUP:]
    edge = (edge + returned.astype(jnp.float32)).astype(jnp.bfloat16)
    grads = jnp.concatenate([inner, edge], axis=1).reshape(-1, width)
    dq = [block.reshape(rows_here, width) for block in dq]
    if paired:
        middles.append(middle(after(rows_of(middle_cuts, 1), inner)))
    near = swap(grads, 1)
    beside = jnp.concatenate([swap(inner, 2), swap(edge, 2)], axis=1).reshape(-1, width)
    if paired:
        far = [ends(after(rows_of(end_cuts, 0), beside, middles[1]))]
        beside = after(beside, near, middles[1])
    grads = [grads, near, beside, swap(beside, 1)]
    dq = [dq[0]] + [swap(after(dq[a], grads[3]), a) for a in range(1, GROUP)]

    if paired:
        in_middle = ((t // 2 == 1) | (t // 2 == 2)).astype(jnp.int32)
        core, y, x = s % 2, s // 2, t % 2
        pos = [here, start, in_middle]
        order = [2 * z + (x ^ a) for z in (core ^ 1, core) for a in range(2)]
        give_own, keep_own = project(pos, order, 2, grads, [(kv_weight, (None, 0, wide, 0))])
        given_own = other_core(give_own)
        far.append(ends(after(rows_of(end_cuts, 1), grads[3])))
        kept, given = [], []
        for lo, hi in zip(end_cuts, end_cuts[1:]):
            parts = []
            for where, weights, cuts in ((1, middles, middle_cuts), (0, far, end_cuts)):
                for weight, first, last in zip(weights, cuts, cuts[1:]):
                    begin, end = max(first, lo), min(last, hi)
                    if begin < end:
                        span = ((begin - first) * unit, (end - begin) * unit, (begin - lo) * unit)
                        parts.append((weight, (where,) + span))
            give_other, keep_other = project(pos, order, 2, grads, parts)
            kept.append(keep_other)
            given.append(other_core(give_other))
        kept[-1] = after(kept[-1], *dq[1:])
        flip = (y ^ group).astype(jnp.int32).reshape(1)
        arrived = deliver(merge(flip, keep_own, given_own, kept, given))
        grad_memory = collect(x.astype(jnp.int32).reshape(1), arrived)
    else:
        weights = [kv_weight] + [
            send(kv_weight, lambda t, s, k=k: ((t + GROUP * k) % n_tgt, s))
            for k in range(1, groups)
        ]
        pos, rows_at = [here, start, 0], list(range(GROUP))
        parts = [project(pos, rows_at, 1, grads, [(w, (None, 0, wide, 0))])[0] for w in weights]
        grad_memory = deliver_any(parts, group)

    here = here.astype(jnp.int32).reshape(1)
    return place_columns(here, dq), grad_memory


def solution(mesh):
    return jax.shard_map(
        per_device,
        mesh=mesh,
        in_specs=(
            P("tgt", "sec"),
            P(None, "tgt", "sec"),
            P("tgt", "sec"),
            P("tgt", None),
            P("tgt"),
            P(None, "tgt", "sec"),
        ),
        out_specs=(P("tgt", "sec"), P("tgt", "sec")),
        check_vma=False,
    )
```

```python
import functools
import math

import jax
import jax.numpy as jnp
from jax import lax
from jax.experimental import pallas as pl
from jax.experimental.pallas import tpu as pltpu
from jax.sharding import PartitionSpec as P

HEAD_DIM = 64
BLOCK = 128
SLOTS = 4
GROUP = 4
AXES = ("tgt", "sec")
SCALE = 0.125
NT = (((1,), (1,)), ((), ()))
TN = (((0,), (0,)), ((), ()))


def send(block, route):
    rows, secs = lax.axis_size("tgt"), lax.axis_size("sec")
    pairs = []
    for t in range(rows):
        for s in range(secs):
            target = route(t, s)
            if target is not None and 0 <= target[0] < rows:
                pairs.append((t * secs + s, target[0] * secs + target[1]))
    return lax.ppermute(block, AXES, pairs)


def swap(block, a):
    return send(block, lambda t, s: (t ^ a, s))


def pack_kernel(total, block_ids, block_count, queries, grad_out, key_values, *outs):
    width = outs[0].shape[1]
    size = queries.shape[0]
    position = lax.axis_index("tgt")
    here, group = lax.rem(position, GROUP), lax.div(position, GROUP)
    blocks_here, slots = block_ids.shape
    shape = (outs[0].shape[0] - 4 * size, width)
    row = lax.broadcasted_iota(jnp.int32, shape, 0)
    column = lax.broadcasted_iota(jnp.int32, shape, 1)
    lists = jnp.zeros(shape, jnp.int32)
    for r in range(blocks_here):
        for n in range(slots):
            slot = lax.rem(block_ids[r, n] - group * GROUP * blocks_here + total, total)
            lists = jnp.where((row == r) & (column == n), slot, lists)
        lists = jnp.where((row == r) & (column == slots), block_count[r], lists)
    lists = lists.astype(jnp.float32).astype(outs[0].dtype)
    for a, out in enumerate(outs):
        columns = pl.ds(pl.multiple_of((here ^ a) * width, width), width)
        out[0:size] = queries[:, columns]
        out[size : 2 * size] = grad_out[:, columns]
        out[2 * size : 3 * size] = key_values[0, :, columns]
        out[3 * size : 4 * size] = key_values[1, :, columns]
        out[4 * size :] = lists


def pack(total, block_ids, block_count, queries, grad_out, key_values):
    width = queries.shape[1] // GROUP
    shape = jax.ShapeDtypeStruct((4 * queries.shape[0] + 16, width), queries.dtype)
    whole = pl.BlockSpec(memory_space=pltpu.VMEM)
    scalars = pl.BlockSpec(memory_space=pltpu.SMEM)
    return pl.pallas_call(
        functools.partial(pack_kernel, total),
        out_shape=[shape] * GROUP,
        in_specs=[scalars] * 2 + [whole] * 3,
        out_specs=[whole] * GROUP,
        name="pack",
    )(block_ids, block_count, queries, grad_out, key_values)


def attend_kernel(span, n_halo, with_halos, with_state, last, meta, pos, *refs):
    packs, refs = refs[:GROUP], refs[GROUP:]
    n_read = n_halo if with_halos else 0
    halos, refs = refs[:n_read], refs[n_read:]
    state, refs = refs[: 2 * with_state], refs[2 * with_state :]
    outs, (keys, values, rows, ups, kg, vg, qm, om) = refs[:-8], refs[-8:]
    acc, dq_all = outs[:2]
    own, width = dq_all.shape[0], dq_all.shape[2]
    per_dev = own // GROUP
    total = own + n_halo * per_dev
    size = per_dev * BLOCK
    heads = width // HEAD_DIM
    here, start = pos[0], pos[1]
    block = (per_dev, BLOCK, width)
    for a in range(GROUP):
        place = pl.ds((here ^ a) * per_dev, per_dev)
        for n, held in enumerate((rows, ups, keys, values)):
            held[place] = packs[a][n * size : (n + 1) * size].reshape(block)
    for n, halo in enumerate(halos):
        part = slice(own + n * per_dev, own + (n + 1) * per_dev)
        keys[part] = halo[:size].reshape(block)
        values[part] = halo[size:].reshape(block)
    if with_state:
        acc[...] = state[0][...]
        dq_all[...] = state[1][...]
    else:
        acc[...] = jnp.zeros_like(acc)
        dq_all[...] = jnp.zeros_like(dq_all)
    lane_head = lax.broadcasted_iota(jnp.int32, (BLOCK, width), 1) // HEAD_DIM
    key_row = lax.broadcasted_iota(jnp.int32, (SLOTS * BLOCK, heads * BLOCK), 0)

    def step(turn, carry):
        member = lax.rem(start + 1 + turn // per_dev, GROUP)
        a = here ^ member
        r = lax.rem(turn, per_dev)
        i = member * per_dev + r
        count = meta[a, r, SLOTS]
        ids = [jnp.clip(meta[a, r, s], 0, total - 1) for s in range(SLOTS)]
        for s in range(SLOTS):
            kg[s * BLOCK : (s + 1) * BLOCK] = keys[ids[s]]
            vg[s * BLOCK : (s + 1) * BLOCK] = values[ids[s]]
        q, o = rows[i], ups[i]
        for h in range(heads):
            qm[h * BLOCK : (h + 1) * BLOCK] = jnp.where(lane_head == h, q, 0)
            om[h * BLOCK : (h + 1) * BLOCK] = jnp.where(lane_head == h, o, 0)
        scores = lax.dot_general(kg[...], qm[...], NT, preferred_element_type=jnp.float32)
        scores = jnp.where(key_row < count * BLOCK, scores, -jnp.inf)
        top = jnp.max(scores, axis=0, keepdims=True)
        expo = jnp.exp2((scores - top) * (SCALE * math.log2(math.e)))
        probs = expo * (1.0 / jnp.sum(expo, axis=0, keepdims=True))
        probs_half = probs.astype(jnp.bfloat16)
        grad_probs = lax.dot_general(vg[...], om[...], NT, preferred_element_type=jnp.float32)
        delta = jnp.sum(probs_half.astype(jnp.float32) * grad_probs, axis=0, keepdims=True)
        grad_half = (probs * (grad_probs - delta)).astype(jnp.bfloat16)
        grad_value = jnp.dot(probs_half, om[...], preferred_element_type=jnp.float32)
        grad_key = SCALE * jnp.dot(grad_half, qm[...], preferred_element_type=jnp.float32)
        for s in range(SLOTS):
            part = slice(s * BLOCK, (s + 1) * BLOCK)
            acc[0, ids[s]] += grad_key[part]
            acc[1, ids[s]] += grad_value[part]
        flipped = lax.dot_general(kg[...], grad_half, TN, preferred_element_type=jnp.float32)
        flipped = jnp.concatenate(
            [
                flipped[h * HEAD_DIM : (h + 1) * HEAD_DIM, h * BLOCK : (h + 1) * BLOCK]
                for h in range(heads)
            ],
            axis=0,
        )
        dq_all[i] = (SCALE * flipped.T).astype(jnp.bfloat16)
        return carry

    lax.fori_loop(span[0], span[1], step, 0)
    half = jnp.bfloat16
    if last:
        dq_outs, (inner, edge) = outs[2 : 2 + GROUP], outs[2 + GROUP :]
        for a in range(GROUP):
            dq_outs[a][...] = dq_all[pl.ds((here ^ a) * per_dev, per_dev)]
        for p in range(GROUP):
            member = lax.rem(start + 1 + p, GROUP)
            taken = acc[:, pl.ds(member * per_dev, per_dev)]
            if p < GROUP - n_halo:
                inner[:, p * per_dev : (p + 1) * per_dev] = taken.astype(half)
            else:
                p -= GROUP - n_halo
                edge[:, p * per_dev : (p + 1) * per_dev] = taken
    elif with_halos:
        for n, back in enumerate(outs[2:]):
            part = slice(own + n * per_dev, own + (n + 1) * per_dev)
            back[...] = acc[:, part].astype(half)


def attend(span, n_halo, meta, pos, packs, halos=(), state=(), last=False):
    per_dev, width = meta.shape[1], packs[0].shape[1]
    own = GROUP * per_dev
    total = own + n_halo * per_dev
    heads = width // HEAD_DIM
    half = jnp.bfloat16
    block = (BLOCK, width)
    shapes = [
        jax.ShapeDtypeStruct((2, total) + block, jnp.float32),
        jax.ShapeDtypeStruct((own,) + block, half),
    ]
    if last:
        shapes += [jax.ShapeDtypeStruct((per_dev,) + block, half)] * GROUP
        shapes.append(jax.ShapeDtypeStruct((2, own - n_halo * per_dev) + block, half))
        shapes.append(jax.ShapeDtypeStruct((2, n_halo * per_dev) + block, jnp.float32))
    elif halos:
        shapes += [jax.ShapeDtypeStruct((2, per_dev) + block, half)] * n_halo
    scratch = (
        [pltpu.VMEM((total,) + block, half)] * 2
        + [pltpu.VMEM((own,) + block, half)] * 2
        + [pltpu.VMEM((SLOTS * BLOCK, width), half)] * 2
        + [pltpu.VMEM((heads * BLOCK, width), half)] * 2
    )
    whole = pl.BlockSpec(memory_space=pltpu.VMEM)
    scalars = pl.BlockSpec(memory_space=pltpu.SMEM)
    turns = span[1] - span[0]
    results = pl.pallas_call(
        functools.partial(attend_kernel, span, n_halo, bool(halos), bool(state), last),
        out_shape=shapes,
        in_specs=[scalars] * 2 + [whole] * (GROUP + len(halos) + len(state)),
        out_specs=[whole] * len(shapes),
        scratch_shapes=scratch,
        compiler_params=pltpu.CompilerParams(vmem_limit_bytes=20 * 2**20),
        cost_estimate=pl.CostEstimate(
            flops=turns * 10 * SLOTS * BLOCK * heads * BLOCK * width,
            bytes_accessed=4 * 2**20,
            transcendentals=turns * SLOTS * heads * BLOCK * BLOCK,
        ),
        name="attend",
    )(meta, pos, *packs, *halos, *state)
    return results[:2], results[2:]


def project_kernel(parts, pos, *refs):
    grads, sources, refs = refs[:GROUP], refs[GROUP : GROUP + len(parts)], refs[GROUP + len(parts) :]
    outs, (total, weights, sems) = refs[:-3], refs[-3:]
    width = grads[0].shape[1]
    rows = grads[0].shape[0] // (2 * GROUP)
    depth = GROUP * width
    per_out = outs[0].shape[0]
    here, start, in_middle = pos[0], pos[1], pos[2]

    def transfer(finish):
        for n, (source, (where, first, size, column)) in enumerate(zip(sources, parts)):

            def move():
                for c in range(2):
                    target = weights.at[c, pl.ds(column, size)]
                    sem = sems.at[n, c]
                    copy = pltpu.make_async_copy(source.at[c, pl.ds(first, size)], target, sem)
                    copy.wait() if finish else copy.start()

            if where is None:
                move()
            else:
                pl.when(in_middle == where)(move)

    transfer(False)
    transfer(True)
    for c in range(2):
        for a in range(GROUP):
            column = pl.multiple_of((here ^ a) * width, width)
            term = lax.dot_general(
                grads[a][c * GROUP * rows : (c + 1) * GROUP * rows],
                weights[c, :, pl.ds(column, width)],
                NT,
                preferred_element_type=jnp.float32,
            )
            total[...] = term if c + a == 0 else total[...] + term
    for n, out in enumerate(outs):
        for j in range(per_out):
            p = lax.rem(pos[3 + n * per_out + j] + (GROUP - 1) - start, GROUP)
            place = pl.ds(pl.multiple_of(p * rows, rows), rows)
            out[j] = total[place].astype(out.dtype)


def project(pos, rows_at, n_out, grads, parts):
    rows = grads[0].shape[0] // (2 * GROUP)
    depth = GROUP * grads[0].shape[1]
    columns = max(column + size for _, (_, _, size, column) in parts)
    half = jnp.bfloat16
    whole = pl.BlockSpec(memory_space=pltpu.VMEM)
    anywhere = pl.BlockSpec(memory_space=pl.ANY)
    count = len(rows_at)
    pos = jnp.stack(list(pos) + list(rows_at)).astype(jnp.int32)
    return pl.pallas_call(
        functools.partial(project_kernel, [part for _, part in parts]),
        out_shape=[jax.ShapeDtypeStruct((count // n_out, rows, columns), half)] * n_out,
        in_specs=[pl.BlockSpec(memory_space=pltpu.SMEM)]
        + [whole] * GROUP
        + [anywhere] * len(parts),
        out_specs=[whole] * n_out,
        scratch_shapes=[
            pltpu.VMEM((GROUP * rows, columns), jnp.float32),
            pltpu.VMEM((2, columns, depth), half),
            pltpu.SemaphoreType.DMA((len(parts), 2)),
        ],
        compiler_params=pltpu.CompilerParams(vmem_limit_bytes=20 * 2**20),
        cost_estimate=pl.CostEstimate(
            flops=4 * count * rows * columns * depth,
            bytes_accessed=6 * 2**20,
            transcendentals=0,
        ),
        name="project",
    )(pos, *grads, *[weight for weight, _ in parts])


def merge_kernel(flip, *refs):
    kept_own, given_own = refs[:2]
    n_parts = (len(refs) - 2 - 4) // 2
    kept, given, outs = refs[2 : 2 + n_parts], refs[2 + n_parts : 2 + 2 * n_parts], refs[-4:]
    for order in range(2):

        @pl.when(flip[0] == order)
        def _():
            for n, out in enumerate(outs):
                if (n % 2) ^ order == 0:
                    terms = [(kept_own, given_own)]
                else:
                    terms = list(zip(kept, given))
                column = 0
                for left, right in terms:
                    size = left.shape[2]
                    total = left[n // 2].astype(jnp.float32) + right[n // 2].astype(jnp.float32)
                    out[:, column : column + size] = total.astype(out.dtype)
                    column += size


def merge(flip, kept_own, given_own, kept, given):
    whole = pl.BlockSpec(memory_space=pltpu.VMEM)
    return pl.pallas_call(
        merge_kernel,
        out_shape=[jax.ShapeDtypeStruct(kept_own.shape[1:], kept_own.dtype)] * 4,
        in_specs=[pl.BlockSpec(memory_space=pltpu.SMEM)] + [whole] * (2 + 2 * len(kept)),
        out_specs=[whole] * 4,
        name="merge",
    )(flip, kept_own, given_own, *kept, *given)


def collect_kernel(pos, *refs):
    parts, out = refs[-2::-1], refs[-1]
    wide = out.shape[1] // 2
    for a in range(2):
        total = parts[2 * a][...].astype(jnp.float32) + parts[2 * a + 1][...].astype(jnp.float32)
        out[:, pl.ds(pl.multiple_of((pos[0] ^ a) * wide, wide), wide)] = total.astype(out.dtype)


def collect(pos, parts):
    rows, wide = parts[0].shape
    whole = pl.BlockSpec(memory_space=pltpu.VMEM)
    return pl.pallas_call(
        collect_kernel,
        out_shape=jax.ShapeDtypeStruct((rows, 2 * wide), parts[0].dtype),
        in_specs=[pl.BlockSpec(memory_space=pltpu.SMEM)] + [whole] * 4,
        out_specs=whole,
        name="collect",
    )(pos, *parts[::-1])


def place_kernel(pos, *refs):
    out = refs[-1]
    for a, part in enumerate(refs[:-1]):
        width = part.shape[1]
        start = pl.multiple_of((pos[0] ^ a) * width, width)
        out[:, pl.ds(start, width)] = part[...]


def place_columns(pos, parts):
    rows, width = parts[0].shape
    whole = pl.BlockSpec(memory_space=pltpu.VMEM)
    return pl.pallas_call(
        place_kernel,
        out_shape=jax.ShapeDtypeStruct((rows, GROUP * width), parts[0].dtype),
        in_specs=[pl.BlockSpec(memory_space=pltpu.SMEM)] + [whole] * len(parts),
        out_specs=whole,
        name="place_columns",
    )(pos, *parts)


def other_core(block):
    return send(block, lambda t, s: (t, s ^ 1))


def deliver(parts):
    arrived = [None] * len(parts)
    for n in reversed(range(len(parts))):
        a1, a2 = n // 2, n % 2

        def route(t, s):
            g, z, x = t // GROUP, (t // 2) % 2, t % 2
            y, core = s // 2, s % 2
            return (g * GROUP + 2 * core + (x ^ a1), 2 * (y ^ a2) + (z ^ y ^ a2 ^ g))

        arrived[n] = send(parts[n], route)
    return arrived


def deliver_any(parts, group):
    groups = len(parts)
    secs = lax.axis_size("sec")
    rows, wide = parts[0].shape[1:]
    stacked = jnp.roll(jnp.stack(parts[::-1]), group + 1, axis=0)
    shape = (secs, groups // secs, GROUP, rows, wide)
    mine = lax.psum_scatter(stacked.reshape(shape), "sec", scatter_dimension=0, tiled=False)
    mine = jnp.moveaxis(mine, 1, 0)
    n_tgt = lax.axis_size("tgt")
    lists = [list(range(g, g + GROUP)) for g in range(0, n_tgt, GROUP)]
    mine = lax.all_to_all(mine, "tgt", 0, 0, axis_index_groups=lists)
    return jnp.transpose(mine, (2, 1, 0, 3)).reshape(rows, -1)


def after(block, *earlier):
    return lax.optimization_barrier((block, *earlier))[0]


def per_device(queries, key_values, grad_out, block_ids, block_count, kv_weight):
    rows_here, width_here = queries.shape
    blocks_here = rows_here // BLOCK
    width = width_here // GROUP
    n_tgt = lax.axis_size("tgt")
    groups = n_tgt // GROUP
    paired = groups == 2
    n_halo = 1 if paired else 2
    t, s = lax.axis_index("tgt"), lax.axis_index("sec")
    group, here = t // GROUP, t % GROUP
    start = jnp.where(group == 0, GROUP - 1, 0) if paired else 0
    pos = jnp.stack([here, start]).astype(jnp.int32)

    def other_group(block):
        return send(block, lambda t, s: (t ^ GROUP, s))

    def middle(block):
        return send(block, lambda t, s: (t ^ 6, s) if t // 2 in (1, 2) else None)

    def ends(block):
        return send(block, lambda t, s: (t ^ 6, s) if t // 2 in (0, 3) else None)

    def shifted(block, k):
        return send(block, lambda t, s: (t + GROUP * k, s))

    wide = kv_weight.shape[1]
    unit = wide // 16
    middle_cuts, end_cuts = (0, 7, 16), (0, 12, 16)

    def rows_of(cuts, n):
        return kv_weight[:, cuts[n] * unit : cuts[n + 1] * unit]

    total = (GROUP + n_halo) * blocks_here
    packs = pack(total, block_ids, block_count, queries, grad_out, key_values)
    if paired:
        middles = [middle(after(rows_of(middle_cuts, 0), packs[0]))]
    packs = [packs[0]] + [swap(packs[a], a) for a in range(1, GROUP)]
    pairs = [p[2 * rows_here : 4 * rows_here] for p in packs]

    def member(m):
        chosen = pairs[0]
        for a in range(1, GROUP):
            chosen = jnp.where(here ^ a == m, pairs[a], chosen)
        return chosen

    if paired:
        halos = [other_group(after(member(start), middles[0]))]
    else:
        halos = [shifted(member(0), -1), shifted(member(GROUP - 1), 1)]

    meta = jnp.stack([p[4 * rows_here : 4 * rows_here + blocks_here, : SLOTS + 1] for p in packs])
    meta = meta.astype(jnp.int32)
    own = GROUP * blocks_here
    n_inner = own - n_halo * blocks_here
    state, _ = attend((0, n_inner // 2), n_halo, meta, pos, packs)
    state, backs = attend((n_inner, own), n_halo, meta, pos, packs, halos, state)
    if paired:
        returned = other_group(backs[0])
    else:
        returned = jnp.concatenate([shifted(backs[1], -1), shifted(backs[0], 1)], axis=1)
    _, results = attend((n_inner // 2, n_inner), n_halo, meta, pos, packs, (), state, True)
    dq, (inner, edge) = results[:GROUP], results[GROUP:]
    edge = (edge + returned.astype(jnp.float32)).astype(jnp.bfloat16)
    grads = jnp.concatenate([inner, edge], axis=1).reshape(-1, width)
    dq = [block.reshape(rows_here, width) for block in dq]
    if paired:
        middles.append(middle(after(rows_of(middle_cuts, 1), inner)))
    near = swap(grads, 1)
    beside = jnp.concatenate([swap(inner, 2), swap(edge, 2)], axis=1).reshape(-1, width)
    if paired:
        far = [ends(after(rows_of(end_cuts, 0), beside, middles[1]))]
        beside = after(beside, near, middles[1])
    grads = [grads, near, beside, swap(beside, 1)]
    dq = [dq[0]] + [swap(after(dq[a], grads[3]), a) for a in range(1, GROUP)]

    if paired:
        in_middle = ((t // 2 == 1) | (t // 2 == 2)).astype(jnp.int32)
        core, y, x = s % 2, s // 2, t % 2
        pos = [here, start, in_middle]
        order = [2 * z + (x ^ a) for z in (core ^ 1, core) for a in range(2)]
        give_own, keep_own = project(pos, order, 2, grads, [(kv_weight, (None, 0, wide, 0))])
        given_own = other_core(give_own)
        far.append(ends(after(rows_of(end_cuts, 1), grads[3])))
        kept, given = [], []
        for lo, hi in zip(end_cuts, end_cuts[1:]):
            parts = []
            for where, weights, cuts in ((1, middles, middle_cuts), (0, far, end_cuts)):
                for weight, first, last in zip(weights, cuts, cuts[1:]):
                    begin, end = max(first, lo), min(last, hi)
                    if begin < end:
                        span = ((begin - first) * unit, (end - begin) * unit, (begin - lo) * unit)
                        parts.append((weight, (where,) + span))
            give_other, keep_other = project(pos, order, 2, grads, parts)
            kept.append(keep_other)
            given.append(other_core(give_other))
        kept[-1] = after(kept[-1], *dq[1:])
        flip = (y ^ group).astype(jnp.int32).reshape(1)
        arrived = deliver(merge(flip, keep_own, given_own, kept, given))
        grad_memory = collect(x.astype(jnp.int32).reshape(1), arrived)
    else:
        weights = [kv_weight] + [
            send(kv_weight, lambda t, s, k=k: ((t + GROUP * k) % n_tgt, s))
            for k in range(1, groups)
        ]
        pos, rows_at = [here, start, 0], list(range(GROUP))
        parts = [project(pos, rows_at, 1, grads, [(w, (None, 0, wide, 0))])[0] for w in weights]
        grad_memory = deliver_any(parts, group)

    here = here.astype(jnp.int32).reshape(1)
    return place_columns(here, dq), grad_memory


def solution(mesh):
    return jax.shard_map(
        per_device,
        mesh=mesh,
        in_specs=(
            P("tgt", "sec"),
            P(None, "tgt", "sec"),
            P("tgt", "sec"),
            P("tgt", None),
            P("tgt"),
            P(None, "tgt", "sec"),
        ),
        out_specs=(P("tgt", "sec"), P("tgt", "sec")),
        check_vma=False,
    )
```

```python
import functools
import math

import jax
import jax.numpy as jnp
from jax import lax
from jax.experimental import pallas as pl
from jax.experimental.pallas import tpu as pltpu
from jax.sharding import PartitionSpec as P

HEAD_DIM = 64
BLOCK = 128
SLOTS = 4
GROUP = 4
AXES = ("tgt", "sec")
SCALE = 0.125
NT = (((1,), (1,)), ((), ()))
TN = (((0,), (0,)), ((), ()))


def send(block, route):
    rows, secs = lax.axis_size("tgt"), lax.axis_size("sec")
    pairs = []
    for t in range(rows):
        for s in range(secs):
            target = route(t, s)
            if target is not None and 0 <= target[0] < rows:
                pairs.append((t * secs + s, target[0] * secs + target[1]))
    return lax.ppermute(block, AXES, pairs)


def swap(block, a):
    return send(block, lambda t, s: (t ^ a, s))


def pack_kernel(total, block_ids, block_count, queries, grad_out, key_values, *outs):
    width = outs[0].shape[1]
    size = queries.shape[0]
    position = lax.axis_index("tgt")
    here, group = lax.rem(position, GROUP), lax.div(position, GROUP)
    blocks_here, slots = block_ids.shape
    shape = (outs[0].shape[0] - 4 * size, width)
    row = lax.broadcasted_iota(jnp.int32, shape, 0)
    column = lax.broadcasted_iota(jnp.int32, shape, 1)
    lists = jnp.zeros(shape, jnp.int32)
    for r in range(blocks_here):
        for n in range(slots):
            slot = lax.rem(block_ids[r, n] - group * GROUP * blocks_here + total, total)
            lists = jnp.where((row == r) & (column == n), slot, lists)
        lists = jnp.where((row == r) & (column == slots), block_count[r], lists)
    lists = lists.astype(jnp.float32).astype(outs[0].dtype)
    for a, out in enumerate(outs):
        columns = pl.ds(pl.multiple_of((here ^ a) * width, width), width)
        out[0:size] = queries[:, columns]
        out[size : 2 * size] = grad_out[:, columns]
        out[2 * size : 3 * size] = key_values[0, :, columns]
        out[3 * size : 4 * size] = key_values[1, :, columns]
        out[4 * size :] = lists


def pack(total, block_ids, block_count, queries, grad_out, key_values):
    width = queries.shape[1] // GROUP
    shape = jax.ShapeDtypeStruct((4 * queries.shape[0] + 16, width), queries.dtype)
    whole = pl.BlockSpec(memory_space=pltpu.VMEM)
    scalars = pl.BlockSpec(memory_space=pltpu.SMEM)
    return pl.pallas_call(
        functools.partial(pack_kernel, total),
        out_shape=[shape] * GROUP,
        in_specs=[scalars] * 2 + [whole] * 3,
        out_specs=[whole] * GROUP,
        name="pack",
    )(block_ids, block_count, queries, grad_out, key_values)


def attend_kernel(span, n_halo, with_halos, with_state, last, meta, pos, *refs):
    packs, refs = refs[:GROUP], refs[GROUP:]
    n_read = n_halo if with_halos else 0
    halos, refs = refs[:n_read], refs[n_read:]
    state, refs = refs[: 2 * with_state], refs[2 * with_state :]
    outs, (keys, values, rows, ups, kg, vg, qm, om) = refs[:-8], refs[-8:]
    acc, dq_all = outs[:2]
    own, width = dq_all.shape[0], dq_all.shape[2]
    per_dev = own // GROUP
    total = own + n_halo * per_dev
    size = per_dev * BLOCK
    heads = width // HEAD_DIM
    here, start = pos[0], pos[1]
    block = (per_dev, BLOCK, width)
    for a in range(GROUP):
        place = pl.ds((here ^ a) * per_dev, per_dev)
        for n, held in enumerate((rows, ups, keys, values)):
            held[place] = packs[a][n * size : (n + 1) * size].reshape(block)
    for n, halo in enumerate(halos):
        part = slice(own + n * per_dev, own + (n + 1) * per_dev)
        keys[part] = halo[:size].reshape(block)
        values[part] = halo[size:].reshape(block)
    if with_state:
        acc[...] = state[0][...]
        dq_all[...] = state[1][...]
    else:
        acc[...] = jnp.zeros_like(acc)
        dq_all[...] = jnp.zeros_like(dq_all)
    lane_head = lax.broadcasted_iota(jnp.int32, (BLOCK, width), 1) // HEAD_DIM
    key_row = lax.broadcasted_iota(jnp.int32, (SLOTS * BLOCK, heads * BLOCK), 0)

    def step(turn, carry):
        member = lax.rem(start + 1 + turn // per_dev, GROUP)
        a = here ^ member
        r = lax.rem(turn, per_dev)
        i = member * per_dev + r
        count = meta[a, r, SLOTS]
        ids = [jnp.clip(meta[a, r, s], 0, total - 1) for s in range(SLOTS)]
        for s in range(SLOTS):
            kg[s * BLOCK : (s + 1) * BLOCK] = keys[ids[s]]
            vg[s * BLOCK : (s + 1) * BLOCK] = values[ids[s]]
        q, o = rows[i], ups[i]
        for h in range(heads):
            qm[h * BLOCK : (h + 1) * BLOCK] = jnp.where(lane_head == h, q, 0)
            om[h * BLOCK : (h + 1) * BLOCK] = jnp.where(lane_head == h, o, 0)
        scores = lax.dot_general(kg[...], qm[...], NT, preferred_element_type=jnp.float32)
        scores = jnp.where(key_row < count * BLOCK, scores, -jnp.inf)
        top = jnp.max(scores, axis=0, keepdims=True)
        expo = jnp.exp2((scores - top) * (SCALE * math.log2(math.e)))
        probs = expo * (1.0 / jnp.sum(expo, axis=0, keepdims=True))
        probs_half = probs.astype(jnp.bfloat16)
        grad_probs = lax.dot_general(vg[...], om[...], NT, preferred_element_type=jnp.float32)
        delta = jnp.sum(probs_half.astype(jnp.float32) * grad_probs, axis=0, keepdims=True)
        grad_half = (probs * (grad_probs - delta)).astype(jnp.bfloat16)
        grad_value = jnp.dot(probs_half, om[...], preferred_element_type=jnp.float32)
        grad_key = SCALE * jnp.dot(grad_half, qm[...], preferred_element_type=jnp.float32)
        for s in range(SLOTS):
            part = slice(s * BLOCK, (s + 1) * BLOCK)
            acc[0, ids[s]] += grad_key[part]
            acc[1, ids[s]] += grad_value[part]
        flipped = lax.dot_general(kg[...], grad_half, TN, preferred_element_type=jnp.float32)
        flipped = jnp.concatenate(
            [
                flipped[h * HEAD_DIM : (h + 1) * HEAD_DIM, h * BLOCK : (h + 1) * BLOCK]
                for h in range(heads)
            ],
            axis=0,
        )
        dq_all[i] = (SCALE * flipped.T).astype(jnp.bfloat16)
        return carry

    lax.fori_loop(span[0], span[1], step, 0)
    half = jnp.bfloat16
    if last:
        dq_outs, (inner, edge) = outs[2 : 2 + GROUP], outs[2 + GROUP :]
        for a in range(GROUP):
            dq_outs[a][...] = dq_all[pl.ds((here ^ a) * per_dev, per_dev)]
        for p in range(GROUP):
            member = lax.rem(start + 1 + p, GROUP)
            taken = acc[:, pl.ds(member * per_dev, per_dev)]
            if p < GROUP - n_halo:
                inner[:, p * per_dev : (p + 1) * per_dev] = taken.astype(half)
            else:
                p -= GROUP - n_halo
                edge[:, p * per_dev : (p + 1) * per_dev] = taken
    elif with_halos:
        for n, back in enumerate(outs[2:]):
            part = slice(own + n * per_dev, own + (n + 1) * per_dev)
            back[...] = acc[:, part].astype(half)


def attend(span, n_halo, meta, pos, packs, halos=(), state=(), last=False):
    per_dev, width = meta.shape[1], packs[0].shape[1]
    own = GROUP * per_dev
    total = own + n_halo * per_dev
    heads = width // HEAD_DIM
    half = jnp.bfloat16
    block = (BLOCK, width)
    shapes = [
        jax.ShapeDtypeStruct((2, total) + block, jnp.float32),
        jax.ShapeDtypeStruct((own,) + block, half),
    ]
    if last:
        shapes += [jax.ShapeDtypeStruct((per_dev,) + block, half)] * GROUP
        shapes.append(jax.ShapeDtypeStruct((2, own - n_halo * per_dev) + block, half))
        shapes.append(jax.ShapeDtypeStruct((2, n_halo * per_dev) + block, jnp.float32))
    elif halos:
        shapes += [jax.ShapeDtypeStruct((2, per_dev) + block, half)] * n_halo
    scratch = (
        [pltpu.VMEM((total,) + block, half)] * 2
        + [pltpu.VMEM((own,) + block, half)] * 2
        + [pltpu.VMEM((SLOTS * BLOCK, width), half)] * 2
        + [pltpu.VMEM((heads * BLOCK, width), half)] * 2
    )
    whole = pl.BlockSpec(memory_space=pltpu.VMEM)
    scalars = pl.BlockSpec(memory_space=pltpu.SMEM)
    turns = span[1] - span[0]
    results = pl.pallas_call(
        functools.partial(attend_kernel, span, n_halo, bool(halos), bool(state), last),
        out_shape=shapes,
        in_specs=[scalars] * 2 + [whole] * (GROUP + len(halos) + len(state)),
        out_specs=[whole] * len(shapes),
        scratch_shapes=scratch,
        compiler_params=pltpu.CompilerParams(vmem_limit_bytes=20 * 2**20),
        cost_estimate=pl.CostEstimate(
            flops=turns * 10 * SLOTS * BLOCK * heads * BLOCK * width,
            bytes_accessed=4 * 2**20,
            transcendentals=turns * SLOTS * heads * BLOCK * BLOCK,
        ),
        name="attend",
    )(meta, pos, *packs, *halos, *state)
    return results[:2], results[2:]


def project_kernel(parts, pos, *refs):
    grads, sources, refs = refs[:GROUP], refs[GROUP : GROUP + len(parts)], refs[GROUP + len(parts) :]
    outs, (total, weights, sems) = refs[:-3], refs[-3:]
    width = grads[0].shape[1]
    rows = grads[0].shape[0] // (2 * GROUP)
    depth = GROUP * width
    per_out = outs[0].shape[0]
    here, start, in_middle = pos[0], pos[1], pos[2]

    def transfer(finish):
        for n, (source, (where, first, size, column)) in enumerate(zip(sources, parts)):

            def move():
                for c in range(2):
                    target = weights.at[c, pl.ds(column, size)]
                    sem = sems.at[n, c]
                    copy = pltpu.make_async_copy(source.at[c, pl.ds(first, size)], target, sem)
                    copy.wait() if finish else copy.start()

            if where is None:
                move()
            else:
                pl.when(in_middle == where)(move)

    transfer(False)
    transfer(True)
    for c in range(2):
        for a in range(GROUP):
            column = pl.multiple_of((here ^ a) * width, width)
            term = lax.dot_general(
                grads[a][c * GROUP * rows : (c + 1) * GROUP * rows],
                weights[c, :, pl.ds(column, width)],
                NT,
                preferred_element_type=jnp.float32,
            )
            total[...] = term if c + a == 0 else total[...] + term
    for n, out in enumerate(outs):
        for j in range(per_out):
            p = lax.rem(pos[3 + n * per_out + j] + (GROUP - 1) - start, GROUP)
            place = pl.ds(pl.multiple_of(p * rows, rows), rows)
            out[j] = total[place].astype(out.dtype)


def project(pos, rows_at, n_out, grads, parts):
    rows = grads[0].shape[0] // (2 * GROUP)
    depth = GROUP * grads[0].shape[1]
    columns = max(column + size for _, (_, _, size, column) in parts)
    half = jnp.bfloat16
    whole = pl.BlockSpec(memory_space=pltpu.VMEM)
    anywhere = pl.BlockSpec(memory_space=pl.ANY)
    count = len(rows_at)
    pos = jnp.stack(list(pos) + list(rows_at)).astype(jnp.int32)
    return pl.pallas_call(
        functools.partial(project_kernel, [part for _, part in parts]),
        out_shape=[jax.ShapeDtypeStruct((count // n_out, rows, columns), half)] * n_out,
        in_specs=[pl.BlockSpec(memory_space=pltpu.SMEM)]
        + [whole] * GROUP
        + [anywhere] * len(parts),
        out_specs=[whole] * n_out,
        scratch_shapes=[
            pltpu.VMEM((GROUP * rows, columns), jnp.float32),
            pltpu.VMEM((2, columns, depth), half),
            pltpu.SemaphoreType.DMA((len(parts), 2)),
        ],
        compiler_params=pltpu.CompilerParams(vmem_limit_bytes=20 * 2**20),
        cost_estimate=pl.CostEstimate(
            flops=4 * count * rows * columns * depth,
            bytes_accessed=6 * 2**20,
            transcendentals=0,
        ),
        name="project",
    )(pos, *grads, *[weight for weight, _ in parts])


def merge_kernel(flip, *refs):
    kept_own, given_own = refs[:2]
    n_parts = (len(refs) - 2 - 4) // 2
    kept, given, outs = refs[2 : 2 + n_parts], refs[2 + n_parts : 2 + 2 * n_parts], refs[-4:]
    for order in range(2):

        @pl.when(flip[0] == order)
        def _():
            for n, out in enumerate(outs):
                if (n % 2) ^ order == 0:
                    terms = [(kept_own, given_own)]
                else:
                    terms = list(zip(kept, given))
                column = 0
                for left, right in terms:
                    size = left.shape[2]
                    total = left[n // 2].astype(jnp.float32) + right[n // 2].astype(jnp.float32)
                    out[:, column : column + size] = total.astype(out.dtype)
                    column += size


def merge(flip, kept_own, given_own, kept, given):
    whole = pl.BlockSpec(memory_space=pltpu.VMEM)
    return pl.pallas_call(
        merge_kernel,
        out_shape=[jax.ShapeDtypeStruct(kept_own.shape[1:], kept_own.dtype)] * 4,
        in_specs=[pl.BlockSpec(memory_space=pltpu.SMEM)] + [whole] * (2 + 2 * len(kept)),
        out_specs=[whole] * 4,
        name="merge",
    )(flip, kept_own, given_own, *kept, *given)


def collect_kernel(pos, *refs):
    parts, out = refs[-2::-1], refs[-1]
    wide = out.shape[1] // 2
    for a in range(2):
        total = parts[2 * a][...].astype(jnp.float32) + parts[2 * a + 1][...].astype(jnp.float32)
        out[:, pl.ds(pl.multiple_of((pos[0] ^ a) * wide, wide), wide)] = total.astype(out.dtype)


def collect(pos, parts):
    rows, wide = parts[0].shape
    whole = pl.BlockSpec(memory_space=pltpu.VMEM)
    return pl.pallas_call(
        collect_kernel,
        out_shape=jax.ShapeDtypeStruct((rows, 2 * wide), parts[0].dtype),
        in_specs=[pl.BlockSpec(memory_space=pltpu.SMEM)] + [whole] * 4,
        out_specs=whole,
        name="collect",
    )(pos, *parts[::-1])


def place_kernel(pos, *refs):
    out = refs[-1]
    for a, part in enumerate(refs[:-1]):
        width = part.shape[1]
        start = pl.multiple_of((pos[0] ^ a) * width, width)
        out[:, pl.ds(start, width)] = part[...]


def place_columns(pos, parts):
    rows, width = parts[0].shape
    whole = pl.BlockSpec(memory_space=pltpu.VMEM)
    return pl.pallas_call(
        place_kernel,
        out_shape=jax.ShapeDtypeStruct((rows, GROUP * width), parts[0].dtype),
        in_specs=[pl.BlockSpec(memory_space=pltpu.SMEM)] + [whole] * len(parts),
        out_specs=whole,
        name="place_columns",
    )(pos, *parts)


def other_core(block):
    return send(block, lambda t, s: (t, s ^ 1))


def deliver(parts):
    arrived = [None] * len(parts)
    for n in reversed(range(len(parts))):
        a1, a2 = n // 2, n % 2

        def route(t, s):
            g, z, x = t // GROUP, (t // 2) % 2, t % 2
            y, core = s // 2, s % 2
            return (g * GROUP + 2 * core + (x ^ a1), 2 * (y ^ a2) + (z ^ y ^ a2 ^ g))

        arrived[n] = send(parts[n], route)
    return arrived


def deliver_any(parts, group):
    groups = len(parts)
    secs = lax.axis_size("sec")
    rows, wide = parts[0].shape[1:]
    stacked = jnp.roll(jnp.stack(parts[::-1]), group + 1, axis=0)
    shape = (secs, groups // secs, GROUP, rows, wide)
    mine = lax.psum_scatter(stacked.reshape(shape), "sec", scatter_dimension=0, tiled=False)
    mine = jnp.moveaxis(mine, 1, 0)
    n_tgt = lax.axis_size("tgt")
    lists = [list(range(g, g + GROUP)) for g in range(0, n_tgt, GROUP)]
    mine = lax.all_to_all(mine, "tgt", 0, 0, axis_index_groups=lists)
    return jnp.transpose(mine, (2, 1, 0, 3)).reshape(rows, -1)


def after(block, *earlier):
    return lax.optimization_barrier((block, *earlier))[0]


def per_device(queries, key_values, grad_out, block_ids, block_count, kv_weight):
    rows_here, width_here = queries.shape
    blocks_here = rows_here // BLOCK
    width = width_here // GROUP
    n_tgt = lax.axis_size("tgt")
    groups = n_tgt // GROUP
    paired = groups == 2
    n_halo = 1 if paired else 2
    t, s = lax.axis_index("tgt"), lax.axis_index("sec")
    group, here = t // GROUP, t % GROUP
    start = jnp.where(group == 0, GROUP - 1, 0) if paired else 0
    pos = jnp.stack([here, start]).astype(jnp.int32)

    def other_group(block):
        return send(block, lambda t, s: (t ^ GROUP, s))

    def middle(block):
        return send(block, lambda t, s: (t ^ 6, s) if t // 2 in (1, 2) else None)

    def ends(block):
        return send(block, lambda t, s: (t ^ 6, s) if t // 2 in (0, 3) else None)

    def shifted(block, k):
        return send(block, lambda t, s: (t + GROUP * k, s))

    wide = kv_weight.shape[1]
    unit = wide // 16
    middle_cuts, end_cuts = (0, 7, 16), (0, 12, 16)

    def rows_of(cuts, n):
        return kv_weight[:, cuts[n] * unit : cuts[n + 1] * unit]

    total = (GROUP + n_halo) * blocks_here
    packs = pack(total, block_ids, block_count, queries, grad_out, key_values)
    if paired:
        middles = [middle(after(rows_of(middle_cuts, 0), packs[0]))]
    packs = [packs[0]] + [swap(packs[a], a) for a in range(1, GROUP)]
    pairs = [p[2 * rows_here : 4 * rows_here] for p in packs]

    def member(m):
        chosen = pairs[0]
        for a in range(1, GROUP):
            chosen = jnp.where(here ^ a == m, pairs[a], chosen)
        return chosen

    if paired:
        halos = [other_group(after(member(start), middles[0]))]
    else:
        halos = [shifted(member(0), -1), shifted(member(GROUP - 1), 1)]

    meta = jnp.stack([p[4 * rows_here : 4 * rows_here + blocks_here, : SLOTS + 1] for p in packs])
    meta = meta.astype(jnp.int32)
    own = GROUP * blocks_here
    n_inner = own - n_halo * blocks_here
    state, _ = attend((0, n_inner // 2), n_halo, meta, pos, packs)
    state, backs = attend((n_inner, own), n_halo, meta, pos, packs, halos, state)
    if paired:
        returned = other_group(backs[0])
    else:
        returned = jnp.concatenate([shifted(backs[1], -1), shifted(backs[0], 1)], axis=1)
    _, results = attend((n_inner // 2, n_inner), n_halo, meta, pos, packs, (), state, True)
    dq, (inner, edge) = results[:GROUP], results[GROUP:]
    edge = (edge + returned.astype(jnp.float32)).astype(jnp.bfloat16)
    grads = jnp.concatenate([inner, edge], axis=1).reshape(-1, width)
    dq = [block.reshape(rows_here, width) for block in dq]
    if paired:
        middles.append(middle(after(rows_of(middle_cuts, 1), inner)))
    near = swap(grads, 1)
    beside = jnp.concatenate([swap(inner, 2), swap(edge, 2)], axis=1).reshape(-1, width)
    if paired:
        far = [ends(after(rows_of(end_cuts, 0), beside, middles[1]))]
        beside = after(beside, near, middles[1])
    grads = [grads, near, beside, swap(beside, 1)]
    dq = [dq[0]] + [swap(after(dq[a], grads[3]), a) for a in range(1, GROUP)]

    if paired:
        in_middle = ((t // 2 == 1) | (t // 2 == 2)).astype(jnp.int32)
        core, y, x = s % 2, s // 2, t % 2
        pos = [here, start, in_middle]
        order = [2 * z + (x ^ a) for z in (core ^ 1, core) for a in range(2)]
        give_own, keep_own = project(pos, order, 2, grads, [(kv_weight, (None, 0, wide, 0))])
        given_own = other_core(give_own)
        far.append(ends(after(rows_of(end_cuts, 1), grads[3])))
        kept, given = [], []
        for lo, hi in zip(end_cuts, end_cuts[1:]):
            parts = []
            for where, weights, cuts in ((1, middles, middle_cuts), (0, far, end_cuts)):
                for weight, first, last in zip(weights, cuts, cuts[1:]):
                    begin, end = max(first, lo), min(last, hi)
                    if begin < end:
                        span = ((begin - first) * unit, (end - begin) * unit, (begin - lo) * unit)
                        parts.append((after(weight, dq[1]), (where,) + span))
            give_other, keep_other = project(pos, order, 2, grads, parts)
            kept.append(keep_other)
            given.append(other_core(give_other))
        kept[-1] = after(kept[-1], *dq[1:])
        flip = (y ^ group).astype(jnp.int32).reshape(1)
        arrived = deliver(merge(flip, keep_own, given_own, kept, given))
        grad_memory = collect(x.astype(jnp.int32).reshape(1), arrived)
    else:
        weights = [kv_weight] + [
            send(kv_weight, lambda t, s, k=k: ((t + GROUP * k) % n_tgt, s))
            for k in range(1, groups)
        ]
        pos, rows_at = [here, start, 0], list(range(GROUP))
        parts = [project(pos, rows_at, 1, grads, [(w, (None, 0, wide, 0))])[0] for w in weights]
        grad_memory = deliver_any(parts, group)

    here = here.astype(jnp.int32).reshape(1)
    return place_columns(here, dq), grad_memory


def solution(mesh):
    return jax.shard_map(
        per_device,
        mesh=mesh,
        in_specs=(
            P("tgt", "sec"),
            P(None, "tgt", "sec"),
            P("tgt", "sec"),
            P("tgt", None),
            P("tgt"),
            P(None, "tgt", "sec"),
        ),
        out_specs=(P("tgt", "sec"), P("tgt", "sec")),
        check_vma=False,
    )
```
